128 devices in a mesh: group: 2 (over x_hi), gx: 8 (over y, core), gy: 8 (over x_lo, z).
Axes of the slice: x: 4 (x_hi: 2, x_lo: 2; x = x_hi * 2 + x_lo), y: 4, z: 4, core: 2. Of those that a mesh axis runs over, the one named last changes fastest.
Arguments:
- domain_state: float32 [2, 100, 128, 2048], P('group', None, 'gx', 'gy'), may hold values from -4 to 4, as said below
- coupling_field: float32 [2, 128, 2048], P('group', 'gx', 'gy'), may hold values from 0 to 1.5
- regime: int32 [128, 2048], P('gx', 'gy'), may hold values from 0 to 2
- land_class: int32 [100, 128, 2048], P(None, 'gx', 'gy'), may hold values from 0 to 7
- flow_code: int32 [100, 128, 2048], P(None, 'gx', 'gy'), may hold values from 0 to 3, as said below
Outputs:
- domain_out: float32 [2, 100, 128, 2048], P('group', None, 'gx', 'gy')
- coupling_out: float32 [2, 128, 2048], P('group', 'gx', 'gy')
The draws below stay inside these ranges and needn't reach their ends.
Inputs may be any that keep to these rules, and one draw needn't show every extreme that they name: `domain_state`: slot 0 channels below 50 hold temperatures, the others moisture between 0.2 and 2; slot 1 holds depths between 0.05 and 2. `regime`: 0 warm rain, 1 mixed phase, 2 deep convection. `flow_code`: codes 0, 1, 2, 3 send a cell's outflow to the next column, next row, previous column, previous row.
All inputs are finite; a program needn't handle non-finite values.
Results may differ from the reference program's by a relative error of at most 0.0003.
Values sent between devices are 32-bit elements; how exact they have to be, the bound alone decides.
No kernel may reach another device: no remote copies, remote signals or barrier semaphores. Data moves between devices by JAX's collectives and lax.ppermute only.
A program may use at most 256 MiB of HBM per device.

```python
import math
import jax
import jax.numpy as jnp

R = 10
LAYER_TOTAL = 50
STEPS = 4
SUB = 12
ATMOS_NORTHWARD_N = 128
ATMOS_EASTWARD_N = 2048


def draw_domain_state(key, part):
    key = jax.random.fold_in(key, 11)
    stochastic_seeds = jax.random.split(key, 3)
    atmos_thermal_state = jnp.clip(jax.random.normal(stochastic_seeds[0], (LAYER_TOTAL, ATMOS_NORTHWARD_N, ATMOS_EASTWARD_N), jnp.float32), -4.0, 4.0)
    specific_moisture = jax.random.uniform(stochastic_seeds[1], (LAYER_TOTAL, ATMOS_NORTHWARD_N, ATMOS_EASTWARD_N), jnp.float32, 0.2, 2.0)
    water_depth = jnp.exp(jax.random.uniform(stochastic_seeds[2], (R * R, ATMOS_NORTHWARD_N, ATMOS_EASTWARD_N), jnp.float32, math.log(0.05), math.log(2.0)))
    atmos_profile_state = jnp.concatenate([atmos_thermal_state, specific_moisture], 0)
    return jnp.stack([atmos_profile_state, water_depth], 0)


def draw_flow_code(key, part):
    key = jax.random.fold_in(key, 23)
    seed_list = jax.random.split(key, 3)
    block_rows = (ATMOS_NORTHWARD_N + 3) // 4
    block_cols = (ATMOS_EASTWARD_N + 3) // 4
    block_dir = jax.random.randint(seed_list[0], (block_rows, block_cols), 0, 4)
    column_dir = jnp.repeat(jnp.repeat(block_dir, 4, axis=0), 4, axis=1)[:ATMOS_NORTHWARD_N, :ATMOS_EASTWARD_N]
    scatter_dir = jax.random.randint(seed_list[1], (R * R, ATMOS_NORTHWARD_N, ATMOS_EASTWARD_N), 0, 4)
    follow = jax.random.randint(seed_list[2], (R * R, ATMOS_NORTHWARD_N, ATMOS_EASTWARD_N), 0, 100) < 88
    return jnp.where(follow, column_dir[None], scatter_dir).astype(jnp.int32)


def plant(array, key, smallest, high):
    extent = array.shape
    index_at = [jax.random.randint(jax.random.fold_in(key, axis), (), 0, extent[axis]) for axis in range(len(extent))]
    array = array.at[tuple(index_at)].set(smallest)
    longest = extent.index(max(extent))
    index_at[longest] = (index_at[longest] + 1) % extent[longest]
    return array.at[tuple(index_at)].set(high)


def shard_levels(key, shape, pieces, smallest, top_value):
    gain, own = 1.0, jax.random.fold_in(key, 6)
    for axis_at, blocks in pieces:
        steps = jnp.exp(jax.random.uniform(jax.random.fold_in(own, axis_at), (blocks,), jnp.float32, smallest / len(pieces), top_value / len(pieces)))
        gain = gain * jnp.repeat(steps, shape[axis_at] // blocks).reshape([-1 if axis == axis_at else 1 for axis in range(len(shape))])
    return gain


def setup_inputs(seed: int = 0) -> dict:
    keys = jax.random.split(jax.random.key(seed), 6)
    domain_state = draw_domain_state(jax.random.fold_in(keys[5], 71), 0)
    coupling_field = jnp.clip(1.5 * jax.random.uniform(keys[1], (2, ATMOS_NORTHWARD_N, ATMOS_EASTWARD_N), jnp.float32) ** shard_levels(keys[1], (2, ATMOS_NORTHWARD_N, ATMOS_EASTWARD_N), ((0, 2), (1, 8), (2, 8)), -0.2, 0.2), 0.0, 1.5)
    regime = plant(jax.random.randint(keys[2], (ATMOS_NORTHWARD_N, ATMOS_EASTWARD_N), 0, 3), jax.random.fold_in(keys[2], 1), 0, 2).astype(jnp.int32)
    land_class = plant(jax.random.randint(keys[3], (R * R, ATMOS_NORTHWARD_N, ATMOS_EASTWARD_N), 0, 8), jax.random.fold_in(keys[3], 1), 0, 7).astype(jnp.int32)
    flow_code = draw_flow_code(jax.random.fold_in(keys[5], 71), 0)
    return {"domain_state": domain_state, "coupling_field": coupling_field, "regime": regime, "land_class": land_class, "flow_code": flow_code}


def atmosphere_step(atmos_profile_state, soil_energy_exchange, regime):
    atmos_thermal_state = atmos_profile_state[:LAYER_TOTAL]
    specific_moisture = atmos_profile_state[LAYER_TOTAL:]
    atmos_thermal_state = jnp.concatenate([atmos_thermal_state[:1] + soil_energy_exchange[None], atmos_thermal_state[1:]], 0)
    specific_moisture = jnp.concatenate([specific_moisture[:1] + soil_energy_exchange[None], specific_moisture[1:]], 0)
    mixing = jnp.where(regime == 2, 0.4, 0.05)[None].astype(jnp.float32)

    def upward_spreading(profile):
        upper_level = jnp.concatenate([profile[1:], profile[-1:]], 0)
        lower_level = jnp.concatenate([profile[:1], profile[:-1]], 0)
        return profile + mixing * (upper_level + lower_level - 2.0 * profile)

    atmos_thermal_state = upward_spreading(atmos_thermal_state)
    specific_moisture = upward_spreading(specific_moisture)
    layer_number = jnp.arange(LAYER_TOTAL, dtype=jnp.float32)
    moisture_capacity = (0.8 * jnp.exp(-3.0 * layer_number / LAYER_TOTAL))[:, None, None] * jnp.exp(0.3 * atmos_thermal_state)
    efficiency = jnp.where(regime == 0, 0.3, jnp.where(regime == 1, 0.6, 0.9))[None].astype(jnp.float32)
    liquid_formed = efficiency * jnp.maximum(specific_moisture - moisture_capacity, 0.0)
    specific_moisture = specific_moisture - liquid_formed
    atmos_thermal_state = atmos_thermal_state + 0.5 * liquid_formed
    rainfall_output = jnp.sum(liquid_formed, axis=0) * (2.0 / LAYER_TOTAL)
    return jnp.concatenate([atmos_thermal_state, specific_moisture], 0), rainfall_output


def to_fine(coarse_field):
    return coarse_field.reshape(R, R, ATMOS_NORTHWARD_N, ATMOS_EASTWARD_N).transpose(2, 0, 3, 1).reshape(ATMOS_NORTHWARD_N * R, ATMOS_EASTWARD_N * R)


def from_fine(fine_field):
    return fine_field.reshape(ATMOS_NORTHWARD_N, R, ATMOS_EASTWARD_N, R).transpose(1, 3, 0, 2).reshape(R * R, ATMOS_NORTHWARD_N, ATMOS_EASTWARD_N)


def routing_step(water, rain_in, outflow_rate, keep_share, direction):
    rain_fine = jnp.repeat(jnp.repeat(rain_in, R, axis=0), R, axis=1)
    water = water + keep_share * rain_fine
    for sub_index in range(SUB):
        outflow = outflow_rate * water * water / (water + 0.5)
        to_east = jnp.where(direction == 0, outflow, 0.0)
        to_south = jnp.where(direction == 1, outflow, 0.0)
        to_west = jnp.where(direction == 2, outflow, 0.0)
        to_north = jnp.where(direction == 3, outflow, 0.0)
        received = jnp.pad(to_east, ((0, 0), (1, 0)))[:, :-1]
        received = received + jnp.pad(to_south, ((1, 0), (0, 0)))[:-1]
        received = received + jnp.pad(to_west, ((0, 0), (0, 1)))[:, 1:]
        received = received + jnp.pad(to_north, ((0, 1), (0, 0)))[1:]
        water = water - outflow + received
    evaporated = 0.1 * water
    water = water - evaporated
    new_flux = evaporated.reshape(ATMOS_NORTHWARD_N, R, ATMOS_EASTWARD_N, R).mean(axis=(1, 3))
    return water, new_flux


def reference(domain_state, coupling_field, regime, land_class, flow_code):
    atmosphere = domain_state[0]
    water = to_fine(domain_state[1])
    land_value = to_fine(land_class).astype(jnp.float32)
    outflow_rate = 0.3 + 0.08 * land_value
    keep_share = 1.0 - (0.6 - 0.07 * land_value)
    direction = to_fine(flow_code)
    soil_energy_exchange = coupling_field[0]
    rain_in = coupling_field[1]
    for step_index in range(STEPS):
        atmosphere, rainfall_output = atmosphere_step(atmosphere, soil_energy_exchange, regime)
        water, new_flux = routing_step(water, rain_in, outflow_rate, keep_share, direction)
        soil_energy_exchange = new_flux
        rain_in = rainfall_output
    domain_out = jnp.stack([atmosphere, from_fine(water)], 0)
    coupling_out = jnp.stack([soil_energy_exchange, rain_in], 0)
    return (domain_out, coupling_out)
```

```python
import functools
import math

import jax
import jax.numpy as jnp
from jax import lax
from jax.experimental import pallas as pl
from jax.experimental.pallas import tpu as pltpu
from jax.sharding import PartitionSpec as P

F32 = jnp.float32
R = 10
LEVELS = 50
STEPS = 4
SUB = 12
NX, NY = 16, 256
HALO = STEPS * SUB
OWN = NX * R
ROWS = OWN + 2 * HALO
TILES = ROWS // 8
MAIN = 2 * R
NCH = MAIN + 2
SVR = ROWS + 16
SHARE = MAIN * OWN
EDGE = MAIN * HALO
CH = 2 * LEVELS + 2
SIDE = CH * 48
STATE = CH * 72
FIRST = (0, 1, 3, 4)
GROUP = (8, 10, 13, 8)
VMEM = pltpu.CompilerParams(vmem_limit_bytes=36 * 1024 * 1024)


def rows8(start):
    return pl.ds(start if isinstance(start, int) else pl.multiple_of(start, 8), 8)


def lanes():
    return lax.broadcasted_iota(jnp.int32, (8, 128), 1)


def picked(x, index):
    return jnp.take_along_axis(x, index, axis=1, mode="promise_in_bounds")


def matmul(a, b):
    return lax.dot_general(
        a, b, (((1,), (0,)), ((), ())), precision=lax.Precision.HIGHEST, preferred_element_type=F32
    )


def loop(n, body):
    def step(i, carry):
        body(i)
        return carry

    lax.fori_loop(0, n, step, 0)


def prep_kernel(info, dom, coup, regime, land, flow, own, pay_a, pay_b):
    even = lax.rem(info[1], 2) == 0

    @pl.when(info[0] == 1)
    def _():
        def one(a):
            for b in range(R):
                c = a * R + b
                for h in range(2):
                    cols = slice(128 * h, 128 * h + 128)
                    land_value = land[c, :, cols].astype(F32)
                    code = flow[c, :, cols]
                    rate = 0.3 + 0.08 * land_value
                    keep = 1.0 - (0.6 - 0.07 * land_value)
                    water = dom[c, :, cols] + keep * coup[:, cols]
                    parts = (
                        2.0 * water + 1.0,
                        jnp.where(code == 0, rate, jnp.where(code == 2, -rate, 0.0)),
                        jnp.where(code == 1, rate, jnp.where(code == 3, -rate, 0.0)),
                    )
                    for k, part in enumerate(parts):
                        at = k * SHARE + (h * R + b) * OWN + a
                        own[pl.ds(at, NX, stride=R), :] = part

        loop(R, one)
        low = jnp.where(even, OWN - HALO, 0)

        def rim(i):
            for t in range(HALO // 8):
                pay_a[rows8(i * HALO + 8 * t), :] = own[rows8(i * OWN + low + 8 * t), :]
                pay_b[rows8(i * HALO + 8 * t), :] = own[rows8(i * OWN + OWN - HALO - low + 8 * t), :]

        loop(3 * MAIN, rim)

    @pl.when(info[0] == 0)
    def _():
        def put(c, load):
            for h in range(2):
                top, bottom = load(0, h), load(8, h)
                own[rows8((c * 2 + h) * 16), :] = top
                own[rows8((c * 2 + h) * 16 + 8), :] = bottom
                pay_a[rows8((c * 2 + h) * 8), :] = jnp.where(even, bottom, top)
                pay_b[rows8((c * 2 + h) * 8), :] = jnp.where(even, top, bottom)

        def one(i):
            for u in range(10):
                c = i * 10 + u
                put(c, lambda r, h: dom[c, r : r + 8, 128 * h : 128 * h + 128])

        loop(10, one)
        put(100, lambda r, h: coup[r : r + 8, 128 * h : 128 * h + 128])
        put(101, lambda r, h: regime[r : r + 8, 128 * h : 128 * h + 128].astype(F32))


def strip_maps():
    lane = lanes()
    left = jnp.maximum(lane - 64, 0)
    right = lane + (NY * R - 64)
    return (left % R, left // R), (right % R, jnp.minimum(right // R - 128, 127))


def gathered(sources, column):
    b_of, y_of = column
    out = picked(sources[0], y_of)
    for b in range(1, R):
        out = jnp.where(b_of == b, picked(sources[b], y_of), out)
    return out


def assemble_kernel(info, own, from_a, from_b, st, rate, r02, r13, sr, pay_c, pay_d):
    even_x = lax.rem(info[1], 2) == 0
    even_y = lax.rem(info[2], 2) == 0
    lane = lanes()

    @pl.when(info[0] == 1)
    def _():
        at_a = jnp.where(even_x, ROWS - HALO, 0)
        at_b = ROWS - HALO - at_a

        def one(c):
            for src, n, at in ((own, OWN, HALO), (from_a, HALO, at_a), (from_b, HALO, at_b)):
                for t in range(n // 8):
                    v, h, w = (src[rows8(k * MAIN * n + c * n + 8 * t), :] for k in range(3))
                    to = rows8(c * ROWS + at + 8 * t)
                    st[to, :] = v if src is own else jnp.where(v == 0.0, 1.0, v)
                    r02[to, :] = h
                    r13[to, :] = w
                    rate[to, :] = jnp.abs(h + w)

        loop(MAIN, one)
        left_of, right_of = strip_maps()

        def strips(t):
            for k, src in enumerate((st, r02, r13)):
                found = []
                for half in range(2):
                    at = 8 * t + 128 * half
                    left = gathered([src[rows8(b * ROWS + at), :] for b in range(R)], left_of)
                    right = gathered([src[rows8((R + b) * ROWS + at), :] for b in range(R)], right_of)
                    found.append((left, right))
                    if k == 0:
                        st[rows8(MAIN * ROWS + at), :] = left
                        st[rows8((MAIN + 1) * ROWS + at), :] = right
                    else:
                        sr[rows8(k * 2 * ROWS + at), :] = left
                        sr[rows8(k * 2 * ROWS + ROWS + at), :] = right
                (l0, q0), (l1, q1) = found
                to_left = jnp.where(lane >= 64, l0, pltpu.roll(l1, 64, 1))
                to_right = jnp.where(lane < 64, q0, pltpu.roll(q1, 64, 1))
                pay_c[rows8(k * 128 + 8 * t), :] = jnp.where(even_y, to_right, to_left)
                pay_d[rows8(k * 128 + 8 * t), :] = jnp.where(even_y, to_left, to_right)

        loop(16, strips)

    @pl.when(info[0] == 0)
    def _():
        sub = lax.broadcasted_iota(jnp.int32, (8, 128), 0)

        def one(i):
            for u in range(6):
                j = i * 6 + u
                st[rows8(j * 24), :] = own[rows8(j * 16), :]
                st[rows8(j * 24 + 8), :] = own[rows8(j * 16 + 8), :]
                a, b = from_a[rows8(j * 8), :], from_b[rows8(j * 8), :]
                above, below = jnp.where(even_x, b, a), jnp.where(even_x, a, b)
                st[rows8(j * 24 + 16), :] = jnp.where(sub >= 4, above, below)

        loop(CH * 2 // 6, one)

        def pack(i):
            k, t = i // 3, i % 3
            to_left = jnp.zeros((8, 128), F32)
            to_right = to_left
            for j in range(32):
                c = jnp.minimum(32 * k + j, CH - 1)
                here = (lane >= 4 * j) & (lane < 4 * j + 4)
                west = st[rows8(c * 48 + 8 * t), :]
                east = st[rows8(c * 48 + 24 + 8 * t), :]
                to_left = jnp.where(here, pltpu.roll(west, 4 * j, 1), to_left)
                to_right = jnp.where(here, pltpu.roll(east, (4 * j + 4) % 128, 1), to_right)
            pay_c[rows8(k * 24 + 8 * t), :] = jnp.where(even_y, to_right, to_left)
            pay_d[rows8(k * 24 + 8 * t), :] = jnp.where(even_y, to_left, to_right)

        loop(12, pack)


def atmosphere_column(src, base, stride, flux, regime, put):
    mixing = jnp.where(regime == 2.0, 0.4, 0.05)
    efficiency = jnp.where(regime == 0.0, 0.3, jnp.where(regime == 1.0, 0.6, 0.9))
    load = lambda c: src[rows8(base + c * stride), :]
    heat, damp = load(0) + flux, load(LEVELS) + flux
    heat_below, damp_below = heat, damp
    total = jnp.zeros((8, 128), F32)
    for k in range(LEVELS):
        last = k == LEVELS - 1
        heat_above = heat if last else load(k + 1)
        damp_above = damp if last else load(LEVELS + k + 1)
        t = heat + mixing * (heat_above + heat_below - 2.0 * heat)
        m = damp + mixing * (damp_above + damp_below - 2.0 * damp)
        capacity = (0.8 * math.exp(-3.0 * k / LEVELS)) * jnp.exp(0.3 * t)
        formed = efficiency * jnp.maximum(m - capacity, 0.0)
        put(k, t + 0.5 * formed)
        put(LEVELS + k, m - formed)
        total = total + formed
        heat_below, damp_below, heat, damp = heat, damp, heat_above, damp_above
    return total * (2.0 / LEVELS)


def coarse_row(shape, coarse_dim):
    fine = lax.broadcasted_iota(jnp.int32, shape, 1 - coarse_dim)
    coarse = lax.broadcasted_iota(jnp.int32, shape, coarse_dim)
    of_fine = (fine + 12) // R - 6
    of_coarse = jnp.where(coarse < 20, coarse, coarse - 24)
    return (of_fine == of_coarse).astype(F32)


def lane_map(strip_dim, right, side):
    strip = lax.broadcasted_iota(jnp.int32, (128, 128), strip_dim)
    lane = lax.broadcasted_iota(jnp.int32, (128, 128), 1 - strip_dim)
    column = (strip + (NY * R - 64)) // R if right else (strip + 16) // R - 8
    if side:
        ours = lane < 4 if right else lane >= 124
        column_of = lane + NY if right else lane - 128
        return ((column == column_of) & ours).astype(F32)
    return (column == (lane + 128 if right else lane)).astype(F32)


def route_kernel(step, *refs):
    opening, closing = step == 0, step == STEPS - 1
    if opening:
        info, st, rate, r02, r13, sr_in, from_c, from_d, new, sr, field = refs[:11]
        scratch = refs[11:]
        fld = None
    else:
        info, st, rate, r02, r13, sr, fld, new, field = refs[:9]
        scratch = refs[9:]
    acc, sv0, sv1, rain, sums = scratch
    even_y = lax.rem(info[2], 2) == 0
    lane = lanes()
    first, count, group = FIRST[step], TILES - 2 * FIRST[step], GROUP[step]

    @pl.when(info[0] == 0)
    def _():
        if opening:

            def side(i):
                k, t = i // 3, i % 3
                c, d = from_c[rows8(k * 24 + 8 * t), :], from_d[rows8(k * 24 + 8 * t), :]
                west, east = jnp.where(even_y, d, c), jnp.where(even_y, c, d)
                for j in range(32):
                    block = jnp.where(
                        lane < 4,
                        pltpu.roll(east, (128 - 4 * j) % 128, 1),
                        jnp.where(lane >= 124, pltpu.roll(west, 124 - 4 * j, 1), 0.0),
                    )

                    @pl.when(32 * k + j < CH)
                    def _():
                        st_side[rows8((32 * k + j) * 24 + 8 * t), :] = block

            st_side = acc
            loop(12, side)

        def block(src, dst, base, to, stride, at):
            flux = src[rows8(base + 100 * stride), :] if opening else fld[rows8(at), :]
            regime = src[rows8(base + 101 * stride), :]

            def put(c, value):
                dst[rows8(to + c * stride), :] = value

            put(101, regime)
            field[rows8(at), :] = atmosphere_column(src, base, stride, flux, regime, put)

        if closing:

            def own(i):
                h, t = i // 2, i % 2
                at = h * 24 + 8 * t
                for u in range(2):

                    @pl.when(h == u)
                    def _():
                        cols = slice(128 * u, 128 * u + 128)

                        def put(c, value):
                            new[c, rows8(8 * t), cols] = value

                        field[rows8(8 * t), cols] = atmosphere_column(
                            st, at, 48, fld[rows8(at), :], st[rows8(at + 101 * 48), :], put
                        )

            loop(4, own)
        else:

            def inner(i):
                at = (i // 3) * 24 + 8 * (i % 3)
                block(st, new, at, at, 48, at)

            def outer(t):
                if opening:
                    block(acc, new, 8 * t, SIDE + 8 * t, 24, 48 + 8 * t)
                else:
                    block(st, new, SIDE + 8 * t, SIDE + 8 * t, 24, 48 + 8 * t)

            loop(6, inner)
            loop(3, outer)

    @pl.when(info[0] == 1)
    def _():
        zero = jnp.zeros((8, 128), F32)
        if opening:

            def side(t):
                for half in range(2):
                    at = 8 * t + 128 * half
                    for k in range(3):
                        c, d = from_c[rows8(k * 128 + 8 * t), :], from_d[rows8(k * 128 + 8 * t), :]
                        west, east = jnp.where(even_y, d, c), jnp.where(even_y, c, d)
                        if half:
                            west, east = pltpu.roll(west, 64, 1), pltpu.roll(east, 64, 1)
                        if k == 0:
                            west = jnp.where(west == 0.0, 1.0, west)
                            east = jnp.where(east == 0.0, 1.0, east)
                            left = st[rows8(MAIN * ROWS + at), :]
                            right = st[rows8((MAIN + 1) * ROWS + at), :]
                        else:
                            left = sr_in[rows8(k * 2 * ROWS + at), :]
                            right = sr_in[rows8(k * 2 * ROWS + ROWS + at), :]
                        left = jnp.where(lane >= 64, left, west)
                        right = jnp.where(lane < 64, right, east)
                        if k == 0:
                            acc[rows8(MAIN * ROWS + at), :] = left
                            acc[rows8((MAIN + 1) * ROWS + at), :] = right
                        else:
                            sr[rows8(k * 2 * ROWS + at), :] = left
                            sr[rows8(k * 2 * ROWS + ROWS + at), :] = right
                    for strip in range(2):
                        a = sr[rows8((2 + strip) * ROWS + at), :]
                        b = sr[rows8((4 + strip) * ROWS + at), :]
                        sr[rows8(strip * ROWS + at), :] = jnp.abs(a + b)

            loop(16, side)

        def rate_of(c, at):
            return rate[rows8(c * ROWS + at), :] if c < MAIN else sr[rows8((c - MAIN) * ROWS + at), :]

        def r02_of(c, at):
            return r02[rows8(c * ROWS + at), :] if c < MAIN else sr[rows8((c - MAIN + 2) * ROWS + at), :]

        def r13_of(c, at):
            return r13[rows8(c * ROWS + at), :] if c < MAIN else sr[rows8((c - MAIN + 4) * ROWS + at), :]

        if opening:

            def fill(t):
                at = 8 * t
                for c in range(MAIN):
                    acc[rows8(c * ROWS + at), :] = st[rows8(c * ROWS + at), :]

        else:
            spread = coarse_row((ROWS, 24), 1)
            blocks = [fld[pl.ds(24 * i, 24), :] for i in range(3)]
            sources = (
                blocks[0],
                blocks[1],
                matmul(blocks[0], lane_map(1, False, False)) + matmul(blocks[2], lane_map(1, False, True)),
                matmul(blocks[1], lane_map(1, True, False)) + matmul(blocks[2], lane_map(1, True, True)),
            )
            for i, source in enumerate(sources):
                rain[pl.ds(i * ROWS, ROWS), :] = matmul(spread, source)

            def fill(t):
                at = 8 * (t + first)
                for c in range(NCH):
                    fall = rain[rows8((c // R if c < MAIN else c - MAIN + 2) * ROWS + at), :]
                    share = 0.275 + 1.75 * rate_of(c, at)
                    acc[rows8(c * ROWS + at), :] = st[rows8(c * ROWS + at), :] + share * fall

        loop(count, fill)

        def clear(t):
            for c in range(NCH):
                sv0[rows8(c * SVR + 8 * (t + first)), :] = zero

        loop(count + 2, clear)
        for c in range(NCH):
            sv1[rows8(c * SVR + 8 * first), :] = zero
            sv1[rows8(c * SVR + 8 * (first + count + 1)), :] = zero

        at_first, at_last = lane == 0, lane == 127

        def settled(sv, c, at):
            row = c * SVR + 8 + at
            above = jnp.maximum(sv[pl.ds(row - 1, 8), :], 0.0)
            below = jnp.minimum(sv[pl.ds(row + 1, 8), :], 0.0)
            return acc[rows8(c * ROWS + at), :] + above - below

        def substep(sv_in, sv_out, i):
            for g in range(group):
                at = 8 * (first + g) + i * (8 * group)

                def cell(c):
                    v = settled(sv_in, c, at)
                    q = (v - 2.0) + pltpu.reciprocal(v, approx=True)
                    sv_out[rows8(c * SVR + 8 + at), :] = r13_of(c, at) * q
                    return v - rate_of(c, at) * q, r02_of(c, at) * q

                heads = [cell(h * R) for h in range(2)]
                tails = [cell(h * R + R - 1) for h in range(2)]
                east = [pltpu.roll(jnp.maximum(x[1], 0.0), 1, 1) for x in tails]
                west = [pltpu.roll(jnp.minimum(x[1], 0.0), 127, 1) for x in heads]
                for c in (MAIN, MAIN + 1):
                    kept, across = cell(c)
                    kept = kept + pltpu.roll(jnp.maximum(across, 0.0), 1, 1)
                    acc[rows8(c * ROWS + at), :] = kept - pltpu.roll(jnp.minimum(across, 0.0), 127, 1)
                for h in range(2):
                    this = heads[h]
                    value = this[0] + jnp.where(at_first, east[1 - h], east[h])
                    for b in range(1, R):
                        after = cell(h * R + b) if b < R - 1 else tails[h]
                        acc[rows8((h * R + b - 1) * ROWS + at), :] = value - jnp.minimum(after[1], 0.0)
                        value = after[0] + jnp.maximum(this[1], 0.0)
                        this = after
                    acc[rows8((h * R + R - 1) * ROWS + at), :] = value - jnp.where(
                        at_last, west[1 - h], west[h]
                    )

        def pair(_):
            loop(count // group, functools.partial(substep, sv0, sv1))
            loop(count // group, functools.partial(substep, sv1, sv0))

        loop(SUB // 2, pair)

        left_of, right_of = strip_maps()
        start = HALO // 8 if closing else FIRST[step + 1]
        for i in range(4 * TILES):
            if not start <= i % TILES < TILES - start:
                sums[rows8(8 * i), :] = zero

        def finish(t):
            at = 8 * (t + start)
            v = [settled(sv0, c, at) for c in range(NCH)]
            for b in range(R):
                place = 10 * lane + b
                inner = jnp.clip(place + 64, 0, 127)
                v[b] = jnp.where(place < SUB, picked(v[MAIN], inner), v[b])
                place = place - (R * 128 - 64)
                inner = jnp.clip(place, 0, 127)
                v[R + b] = jnp.where(place >= 64 - SUB, picked(v[MAIN + 1], inner), v[R + b])
            for h in range(2):
                total = v[h * R]
                for b in range(1, R):
                    total = total + v[h * R + b]
                sums[rows8(h * ROWS + at), :] = total - float(R)
            if not closing:
                v[MAIN] = jnp.where(lane >= 64 + SUB, gathered(v[:R], left_of), v[MAIN])
                v[MAIN + 1] = jnp.where(lane < 64 - SUB, gathered(v[R:MAIN], right_of), v[MAIN + 1])
                sums[rows8(2 * ROWS + at), :] = v[MAIN] - 1.0
                sums[rows8(3 * ROWS + at), :] = v[MAIN + 1] - 1.0
                for c in range(NCH):
                    new[rows8(c * ROWS + at), :] = 0.9 * v[c] + 0.1
            else:
                for c in range(MAIN):
                    acc[rows8(c * ROWS + at), :] = 0.45 * (v[c] - 1.0)

        loop(TILES - 2 * start, finish)
        pool = coarse_row((24, ROWS), 0)
        parts = [matmul(pool, sums[pl.ds(i * ROWS, ROWS), :]) for i in range(2 if closing else 4)]
        scale = 0.1 / (2.0 * R * R)
        if closing:
            for h in range(2):
                field[:, 128 * h : 128 * h + 128] = parts[h][:NX] * scale

            def lay(a):
                for b in range(R):
                    for h in range(2):
                        new[a * R + b, :, 128 * h : 128 * h + 128] = acc[
                            pl.ds((h * R + b) * ROWS + HALO + a, NX, stride=R), :
                        ]

            loop(R, lay)
        else:
            field[pl.ds(0, 24), :] = parts[0] * scale
            field[pl.ds(24, 24), :] = parts[1] * scale
            side_part = matmul(parts[2], lane_map(0, False, True)) + matmul(parts[3], lane_map(0, True, True))
            field[pl.ds(48, 24), :] = side_part * scale


def shapes(*sizes):
    return [jax.ShapeDtypeStruct(s if isinstance(s, tuple) else (s, 128), F32) for s in sizes]


def call(kernel, args, out, scratch=()):
    in_specs = [pl.BlockSpec(memory_space=pltpu.SMEM)]
    in_specs += [pl.BlockSpec(memory_space=pltpu.VMEM)] * (len(args) - 1)
    return pl.pallas_call(
        kernel,
        out_shape=shapes(*out),
        in_specs=in_specs,
        out_specs=[pl.BlockSpec(memory_space=pltpu.VMEM)] * len(out),
        scratch_shapes=[pltpu.VMEM((n, 128), F32) for n in scratch],
        compiler_params=VMEM,
    )(*args)


def pairs(axis, odd):
    n = lax.axis_size(axis)
    found = [(i, i + 1) for i in range(odd, n - 1, 2)]
    return found + [(j, i) for i, j in found]


def on_device(domain_state, coupling_field, regime, land_class, flow_code):
    info = jnp.stack([lax.axis_index(a) for a in ("group", "gx", "gy")]).astype(jnp.int32)
    args = (info, domain_state[0], coupling_field[0], regime, land_class, flow_code)
    own, pay_a, pay_b = call(prep_kernel, args, (3 * SHARE, 3 * EDGE, 3 * EDGE))
    from_a = lax.ppermute(pay_a, "gx", pairs("gx", 0))
    from_b = lax.ppermute(pay_b, "gx", pairs("gx", 1))
    full = MAIN * ROWS
    st, rate, r02, r13, sr, pay_c, pay_d = call(
        assemble_kernel,
        (info, own, from_a, from_b),
        (STATE, full, full, full, 6 * ROWS, 384, 384),
    )
    from_c = lax.ppermute(pay_c, "gy", pairs("gy", 0))
    from_d = lax.ppermute(pay_d, "gy", pairs("gy", 1))
    scratch = (NCH * ROWS, NCH * SVR, NCH * SVR, 4 * ROWS, 4 * ROWS)
    for step in range(STEPS):
        kernel = functools.partial(route_kernel, step)
        if step == 0:
            st, sr, field = call(
                kernel, (info, st, rate, r02, r13, sr, from_c, from_d), (STATE, 6 * ROWS, 72), scratch
            )
        elif step < STEPS - 1:
            st, field = call(kernel, (info, st, rate, r02, r13, sr, field), (STATE, 72), scratch)
        else:
            out, field = call(
                kernel,
                (info, st, rate, r02, r13, sr, field),
                ((2 * LEVELS, NX, NY), (NX, NY)),
                scratch,
            )
        field = lax.ppermute(field, "group", [(0, 1), (1, 0)])
    return (out[None], field[None])


def solution(mesh):
    return jax.shard_map(
        on_device,
        mesh=mesh,
        in_specs=(
            P("group", None, "gx", "gy"),
            P("group", "gx", "gy"),
            P("gx", "gy"),
            P(None, "gx", "gy"),
            P(None, "gx", "gy"),
        ),
        out_specs=(P("group", None, "gx", "gy"), P("group", "gx", "gy")),
        check_vma=False,
    )
```

```python
import functools
import math

import jax
import jax.numpy as jnp
from jax import lax
from jax.experimental import pallas as pl
from jax.experimental.pallas import tpu as pltpu
from jax.sharding import PartitionSpec as P

F32 = jnp.float32
R = 10
LEVELS = 50
STEPS = 4
SUB = 12
NX, NY = 16, 256
HALO = STEPS * SUB
OWN = NX * R
ROWS = OWN + 2 * HALO
TILES = ROWS // 8
MAIN = 2 * R
NCH = MAIN + 2
SVR = ROWS + 16
EDGE = MAIN * HALO
CH = 2 * LEVELS + 2
RANGES = (
    ((0, 8, 12),),
    ((1, 10, 4), (2, 14, 8)),
    ((3, 13, 8), (4, 8, 4)),
    ((4, 8, 4), (5, 11, 8)),
)
MIB = 1024 * 1024
EDGE_TILES = 9


def rows8(start):
    return pl.ds(start if isinstance(start, int) else pl.multiple_of(start, 8), 8)


def lanes():
    return lax.broadcasted_iota(jnp.int32, (8, 128), 1)


def picked(x, index):
    return jnp.take_along_axis(x, index, axis=1, mode="promise_in_bounds")


def loop(n, body):
    def step(i, carry):
        body(i)
        return carry

    lax.fori_loop(0, n, step, 0)


def info_of():
    return [lax.axis_index(a) for a in ("group", "gx", "gy")]


class Inputs:
    def __init__(self, hbm, vmem, sems, sems2):
        self.dom, self.coup, self.regime, self.land, self.flow = vmem
        self.big = [(hbm[i], vmem[i]) for i in (0, 3, 4)]
        self.small = [pltpu.make_async_copy(hbm[i], vmem[i], sems2.at[i - 1]) for i in (1, 2)]
        self.sems = sems

    def part(self, k, i):
        src, dst = self.big[k]
        cut = pl.ds(i * R, R)
        return pltpu.make_async_copy(src.at[cut], dst.at[cut], self.sems.at[k, i])

    def start(self, kinds):
        for x in self.small:
            x.start()
        for i in range(R):
            for k in range(kinds):
                self.part(k, i).start()
        for x in self.small:
            x.wait()

    def wait(self, kinds, i):
        for k in range(kinds):
            self.part(k, i).wait()

    def lay_out(self, put):
        self.start(3)

        def one(a):
            self.wait(3, a)
            for b in range(R):
                c = a * R + b
                for h in range(2):
                    cols = slice(128 * h, 128 * h + 128)
                    land_value = self.land[c, :, cols].astype(F32)
                    code = self.flow[c, :, cols]
                    rate = 0.3 + 0.08 * land_value
                    keep = 1.0 - (0.6 - 0.07 * land_value)
                    water = self.dom[c, :, cols] + keep * self.coup[:, cols]
                    put(0, h * R + b, a, 2.0 * water + 1.0)
                    put(1, h * R + b, a, jnp.where(code == 0, rate, jnp.where(code == 2, -rate, 0.0)))
                    put(2, h * R + b, a, jnp.where(code == 1, rate, jnp.where(code == 3, -rate, 0.0)))

        loop(R, one)

    def blocks(self, put):
        self.start(1)

        def one(i):
            self.wait(1, i)
            for u in range(10):
                for h in range(2):
                    for t in range(2):
                        put(i * 10 + u, h, t, self.dom[i * 10 + u, 8 * t : 8 * t + 8, 128 * h : 128 * h + 128])

        loop(R, one)
        for h in range(2):
            for t in range(2):
                cut = (slice(8 * t, 8 * t + 8), slice(128 * h, 128 * h + 128))
                put(100, h, t, self.coup[cut])
                put(101, h, t, self.regime[cut].astype(F32))


def prep_kernel(*refs):
    pay_a, pay_b, own = refs[5], refs[6], refs[14]
    inputs = Inputs(refs[:5], refs[7:12], *refs[12:14])
    group, gx, _ = info_of()
    even = lax.rem(gx, 2) == 0

    @pl.when(group == 1)
    def _():
        def put(k, c, a, value):
            own[k * MAIN + c, pl.ds(a, NX, stride=R), :] = value

        inputs.lay_out(put)
        low = jnp.where(even, OWN - HALO, 0)

        def rim(i):
            for t in range(HALO // 8):
                pay_a[rows8(i * HALO + 8 * t), :] = own[i, rows8(low + 8 * t), :]
                pay_b[rows8(i * HALO + 8 * t), :] = own[i, rows8(OWN - HALO - low + 8 * t), :]

        loop(3 * MAIN, rim)

    @pl.when(group == 0)
    def _():
        def put(c, h, t, value):
            @pl.when(even == (t == 1))
            def _():
                pay_a[rows8((c * 2 + h) * 8), :] = value

            @pl.when(even == (t == 0))
            def _():
                pay_b[rows8((c * 2 + h) * 8), :] = value

        inputs.blocks(put)


def early_kernel(*refs):
    stw, sta, r02, r13, inner = refs[5:10]
    inputs = Inputs(refs[:5], refs[10:15], *refs[15:17])
    acc, sv0, sv1 = refs[17:]
    group, _, _ = info_of()

    @pl.when(group == 1)
    def _():
        def put(k, c, a, value):
            (stw, r02, r13)[k][c, pl.ds(HALO + a, NX, stride=R), :] = value

        inputs.lay_out(put)
        begin, size = HALO // 8, 10

        def fill(t):
            here = rows8(8 * (t + begin))
            for c in range(MAIN):
                acc[c, here, :] = stw[c, here, :]

        loop(OWN // 8, fill)
        zero = jnp.zeros((8, 128), F32)

        def clear(t):
            for c in range(MAIN):
                sv0[c, rows8(8 * (t + begin)), :] = zero

        loop(OWN // 8 + 2, clear)
        for c in range(MAIN):
            sv1[c, rows8(8 * begin), :] = zero
            sv1[c, rows8(HALO + OWN + 8), :] = zero
        flow = Flow(acc, lambda k, c, here: (r02, r13)[k][c, here, :])

        def pair(_):
            loop(OWN // (8 * size), functools.partial(flow.substep, begin, size, sv0, sv1, range(2), ()))
            loop(OWN // (8 * size), functools.partial(flow.substep, begin, size, sv1, sv0, range(2), ()))

        loop(SUB // 2, pair)

        def finish(t):
            for u in range(2):
                at = 16 * t + HALO + 8 * u
                for c in range(MAIN):
                    inner[c, rows8(at), :] = flow.settled(sv0, c, at)

        loop(OWN // 16, finish)

    @pl.when(group == 0)
    def _():
        def put(c, h, t, value):
            sta[c, 24 * h + 8 * t : 24 * h + 8 * t + 8, :] = value

        inputs.blocks(put)


class Flow:
    def __init__(self, acc, rate):
        self.acc, self.rate = acc, rate

    def settled(self, sv, c, at):
        above = jnp.maximum(sv[c, pl.ds(at + 7, 8), :], 0.0)
        below = jnp.minimum(sv[c, pl.ds(at + 9, 8), :], 0.0)
        return self.acc[c, rows8(at), :] + above - below

    def substep(self, begin, group, sv_in, sv_out, halves, strips, i):
        acc, lane = self.acc, lanes()
        start = pl.multiple_of(i * (8 * group), 8) + 8 * begin
        for g in range(group):
            at = start + 8 * g
            here = rows8(at)

            def cell(c):
                v = self.settled(sv_in, c, at)
                q = (v - 2.0) + pltpu.reciprocal(v, approx=True)
                down, across = self.rate(1, c, here) * q, self.rate(0, c, here) * q
                sv_out[c, rows8(at + 8), :] = down
                return v - jnp.abs(down + across), across

            heads = [cell(h * R) for h in halves]
            tails = [cell(h * R + R - 1) for h in halves]
            east = [pltpu.roll(jnp.maximum(x[1], 0.0), 1, 1) for x in tails]
            west = [pltpu.roll(jnp.minimum(x[1], 0.0), 127, 1) for x in heads]
            for c in strips:
                kept, across = cell(c)
                kept = kept + pltpu.roll(jnp.maximum(across, 0.0), 1, 1)
                acc[c, here, :] = kept - pltpu.roll(jnp.minimum(across, 0.0), 127, 1)
            for h in halves:
                this = heads[h]
                value = this[0] + jnp.where(lane == 0, east[1 - h], east[h])
                for b in range(1, R):
                    after = cell(h * R + b) if b < R - 1 else tails[h]
                    acc[h * R + b - 1, here, :] = value - jnp.minimum(after[1], 0.0)
                    value = after[0] + jnp.maximum(this[1], 0.0)
                    this = after
                acc[h * R + R - 1, here, :] = value - jnp.where(lane == 127, west[1 - h], west[h])


def strip_map():
    lane = lanes()
    fine = jnp.where(lane >= 64, lane - 64, lane + (NY * R - 64))
    return fine % R, fine // R % 128


def gathered(left, right, column):
    b_of, y_of = column
    near_left = lanes() < 64
    out = None
    for b in range(R):
        found = picked(jnp.where(near_left, left[b], right[b]), y_of)
        out = found if b == 0 else jnp.where(b_of == b, found, out)
    return out


def assemble_kernel(stw_in, sta_in, r02_in, r13_in, from_a, from_b, stw, sta, r02, r13, sr, pay_c, pay_d):
    group, gx, gy = info_of()
    even_x, even_y = lax.rem(gx, 2) == 0, lax.rem(gy, 2) == 0
    lane = lanes()

    @pl.when(group == 1)
    def _():
        at_a = jnp.where(even_x, ROWS - HALO, 0)
        at_b = ROWS - HALO - at_a

        def one(c):
            def join(v, h, w, to):
                stw[c, to, :] = v
                r02[c, to, :] = h
                r13[c, to, :] = w

            for t in range(OWN // 8):
                here = rows8(HALO + 8 * t)
                join(stw_in[c, here, :], r02_in[c, here, :], r13_in[c, here, :], here)
            for src, at in ((from_a, at_a), (from_b, at_b)):
                for t in range(HALO // 8):
                    v, h, w = (src[rows8((k * MAIN + c) * HALO + 8 * t), :] for k in range(3))
                    join(jnp.where(v == 0.0, 1.0, v), h, w, rows8(at + 8 * t))

        loop(MAIN, one)
        column = strip_map()

        def strips(t):
            for k, src in enumerate((stw, r02, r13)):
                found = []
                for half in range(2):
                    here = rows8(8 * t + 128 * half)
                    got = gathered([src[b, here, :] for b in range(R)], [src[R + b, here, :] for b in range(R)], column)
                    found.append(got)
                    if k == 0:
                        stw[MAIN, here, :] = got
                    else:
                        sr[2 * k - 2, here, :] = got
                one, two = found
                turned = pltpu.roll(two, 64, 1)
                to_left = jnp.where(lane >= 64, one, turned)
                to_right = jnp.where(lane < 64, one, turned)
                pay_c[rows8(k * 128 + 8 * t), :] = jnp.where(even_y, to_right, to_left)
                pay_d[rows8(k * 128 + 8 * t), :] = jnp.where(even_y, to_left, to_right)

        loop(16, strips)

    @pl.when(group == 0)
    def _():
        sub = lax.broadcasted_iota(jnp.int32, (8, 128), 0)

        def one(c):
            for h in range(2):
                for t in range(2):
                    here = slice(24 * h + 8 * t, 24 * h + 8 * t + 8)
                    sta[c, here, :] = sta_in[c, here, :]
                a, b = (x[rows8((c * 2 + h) * 8), :] for x in (from_a, from_b))
                above, below = jnp.where(even_x, b, a), jnp.where(even_x, a, b)
                sta[c, 24 * h + 16 : 24 * h + 24, :] = jnp.where(sub >= 4, above, below)

        loop(CH, one)

        def pack(i):
            k, t = i // 3, lax.rem(i, 3)
            to_left = jnp.zeros((8, 128), F32)
            to_right = to_left
            for j in range(32):
                c = jnp.minimum(32 * k + j, CH - 1)
                here = (lane >= 4 * j) & (lane < 4 * j + 4)
                west = sta[c, rows8(8 * t), :]
                east = sta[c, rows8(24 + 8 * t), :]
                to_left = jnp.where(here, pltpu.roll(west, 4 * j, 1), to_left)
                to_right = jnp.where(here, pltpu.roll(east, (4 * j + 4) % 128, 1), to_right)
            pay_c[rows8(k * 24 + 8 * t), :] = jnp.where(even_y, to_right, to_left)
            pay_d[rows8(k * 24 + 8 * t), :] = jnp.where(even_y, to_left, to_right)

        loop(12, pack)


def atmosphere_column(load, flux, regime, put):
    mixing = jnp.where(regime == 2.0, 0.4, 0.05)
    efficiency = jnp.where(regime == 0.0, 0.3, jnp.where(regime == 1.0, 0.6, 0.9))
    heat, damp = load(0) + flux, load(LEVELS) + flux
    heat_below, damp_below = heat, damp
    total = jnp.zeros((8, 128), F32)
    for k in range(LEVELS):
        last = k == LEVELS - 1
        heat_above = heat if last else load(k + 1)
        damp_above = damp if last else load(LEVELS + k + 1)
        t = heat + mixing * (heat_above + heat_below - 2.0 * heat)
        m = damp + mixing * (damp_above + damp_below - 2.0 * damp)
        capacity = (0.8 * math.exp(-3.0 * k / LEVELS)) * jnp.exp(0.3 * t)
        formed = efficiency * jnp.maximum(m - capacity, 0.0)
        put(k, t + 0.5 * formed)
        put(LEVELS + k, m - formed)
        total = total + formed
        heat_below, damp_below, heat, damp = heat, damp, heat_above, damp_above
    return total * (2.0 / LEVELS)


BANDS = ((0, 16, HALO), (16, 4, HALO + OWN), (20, 4, HALO - 4 * R))


def strip_rain(h0, h1, side, t):
    lane = lanes()
    here = slice(8 * t, 8 * t + 8)
    y = (lane + 16) // R - 8
    left = jnp.where(
        y < 0, picked(side[here], jnp.clip(128 + y, 0, 127)), picked(h0[here], jnp.clip(y, 0, 127))
    )
    y = (lane + (NY * R - 64)) // R
    right = jnp.where(
        y < NY, picked(h1[here], jnp.clip(y - 128, 0, 127)), picked(side[here], jnp.clip(y - NY, 0, 127))
    )
    return left, right


def strip_flux(left, right):
    lane = lanes()
    out = []
    for x, start in (
        (left, jnp.where(lane < 64, 64 + R * lane, 64 + R * (lane - 128))),
        (right, jnp.where(lane < 64, 64 + R * lane, 64 + R * (lane - 128))),
    ):
        back = lambda v, n: pltpu.roll(v, 128 - n, 1)
        two = x + back(x, 1)
        four = two + back(two, 2)
        ten = four + back(four, 4) + back(two, 8)
        out.append(picked(ten, jnp.clip(start, 0, 127)))
    return out


def route_kernel(step, *refs):
    opening, closing = step == 0, step == STEPS - 1
    if opening:
        stw, sta, r02, r13, sr_in, done, from_c, from_d, new, new_a, sr, field = refs[:12]
        acc, sv0, sv1, rain, sums, side_a = refs[12:]
        fld = None
    elif closing:
        stw, sta, r02, r13, sr, fld, out, field = refs[:8]
        acc, sv0, sv1, rain, sums = refs[8:]
    else:
        stw, sta, r02, r13, sr, fld, new, new_a, field = refs[:9]
        acc, sv0, sv1, rain, sums = refs[9:]
    group, _, gy = info_of()
    even_y = lax.rem(gy, 2) == 0
    lane = lanes()
    ranges = RANGES[step]
    first = ranges[0][0]
    count = TILES - 2 * first

    @pl.when(group == 0)
    def _():
        if opening:

            def side(i):
                k, t = i // 3, lax.rem(i, 3)
                c, d = from_c[rows8(k * 24 + 8 * t), :], from_d[rows8(k * 24 + 8 * t), :]
                west, east = jnp.where(even_y, d, c), jnp.where(even_y, c, d)
                for j in range(32):
                    side_a[32 * k + j, rows8(8 * t), :] = jnp.where(
                        lane < 4,
                        pltpu.roll(east, (128 - 4 * j) % 128, 1),
                        jnp.where(lane >= 124, pltpu.roll(west, 124 - 4 * j, 1), 0.0),
                    )

            loop(12, side)

        if closing:

            def own(i):
                h, t = i // 2, lax.rem(i, 2)
                here = rows8(24 * h + 8 * t)
                for u in range(2):

                    @pl.when(h == u)
                    def _():
                        cols = slice(128 * u, 128 * u + 128)

                        def put(c, value):
                            out[c, rows8(8 * t), cols] = value

                        field[rows8(8 * t), cols] = atmosphere_column(
                            lambda c: sta[c, here, :], fld[here, :], sta[CH - 1, here, :], put
                        )

            loop(4, own)
        else:

            def block(load, here):
                def put(c, value):
                    new_a[c, here, :] = value

                regime = load(CH - 1)
                put(CH - 1, regime)
                flux = load(CH - 2) if opening else fld[here, :]
                field[here, :] = atmosphere_column(load, flux, regime, put)

            def inner(i):
                here = rows8(8 * i)
                block(lambda c: sta[c, here, :], here)

            def outer(t):
                block(lambda c: side_a[c, rows8(8 * t), :], rows8(48 + 8 * t))

            if opening:
                loop(6, inner)
                loop(3, outer)
            else:
                loop(9, inner)

    @pl.when(group == 1)
    def _():
        zero = jnp.zeros((8, 128), F32)
        if opening:

            def side(t):
                for half in range(2):
                    here = rows8(8 * t + 128 * half)
                    for k in range(3):
                        c, d = from_c[rows8(k * 128 + 8 * t), :], from_d[rows8(k * 128 + 8 * t), :]
                        west, east = jnp.where(even_y, d, c), jnp.where(even_y, c, d)
                        if half:
                            west, east = pltpu.roll(west, 64, 1), pltpu.roll(east, 64, 1)
                        if k == 0:
                            west = jnp.where(west == 0.0, 1.0, west)
                            east = jnp.where(east == 0.0, 1.0, east)
                        inner = sr_in[2 * k - 2, here, :] if k else stw[MAIN, here, :]
                        left = jnp.where(lane >= 64, inner, west)
                        right = jnp.where(lane < 64, inner, east)
                        if k == 0:
                            acc[MAIN, here, :] = left
                            acc[MAIN + 1, here, :] = right
                        else:
                            sr[2 * k - 2, here, :] = left
                            sr[2 * k - 1, here, :] = right

            loop(16, side)

        def of(main, k, c, here):
            return main[c, here, :] if c < MAIN else sr[2 * k + c - MAIN, here, :]

        if opening:

            def fill(t):
                for at in (8 * t, 8 * t + 8 * (TILES - EDGE_TILES)):
                    for c in range(MAIN):
                        acc[c, rows8(at), :] = stw[c, rows8(at), :]

        else:
            blocks = [fld[pl.ds(24 * i, 24), :] for i in range(3)]
            found = [strip_rain(*blocks, t) for t in range(3)]
            for at, n, fine in BANDS:
                if n == 16:
                    pieces = [b[:16] for b in blocks[:2]]
                    pieces += [jnp.concatenate([found[0][i], found[1][i]], 0) for i in range(2)]
                else:
                    cut = slice(at - 16, at - 12)
                    pieces = [b[at : at + 4] for b in blocks[:2]] + [found[2][i][cut] for i in range(2)]
                for i, piece in enumerate(pieces):
                    for a in range(R):
                        rain[i, pl.ds(fine + a, n, stride=R), :] = piece

            def fill(t):
                here = rows8(8 * (t + first))
                for c in range(NCH):
                    fall = rain[c // R if c < MAIN else c - MAIN + 2, here, :]
                    rate = jnp.abs(of(r02, 0, c, here) + of(r13, 1, c, here))
                    share = 0.275 + 1.75 * rate
                    acc[c, here, :] = stw[c, here, :] + share * fall

        loop(EDGE_TILES if opening else count, fill)

        def clear(t):
            for c in range(NCH):
                sv0[c, rows8(8 * (t + first)), :] = zero

        loop(count + 2, clear)
        for c in range(NCH):
            sv1[c, rows8(8 * first), :] = zero
            sv1[c, rows8(8 * (first + count + 1)), :] = zero

        flow = Flow(acc, lambda k, c, here: of((r02, r13)[k], k, c, here))
        strips = (MAIN, MAIN + 1)
        if opening:
            for c in range(MAIN):
                sv1[c, rows8(8 * (EDGE_TILES + 1)), :] = zero
                sv1[c, rows8(8 * (TILES - EDGE_TILES)), :] = zero

            def pair(_):
                for sv in ((sv0, sv1), (sv1, sv0)):
                    flow.substep(0, EDGE_TILES, *sv, range(2), (), 0)
                    flow.substep(TILES - EDGE_TILES, EDGE_TILES, *sv, range(2), (), 0)
                    loop(2, functools.partial(flow.substep, 0, TILES // 2, *sv, (), strips))

            loop(SUB // 2, pair)
        else:
            for begin, size, substeps in ranges:

                def pair(_):
                    times = (TILES - 2 * begin) // size
                    loop(times, functools.partial(flow.substep, begin, size, sv0, sv1, range(2), strips))
                    loop(times, functools.partial(flow.substep, begin, size, sv1, sv0, range(2), strips))

                loop(substeps // 2, pair)

        column = strip_map()
        start = HALO // 8 if closing else RANGES[step + 1][0][0]
        near_left = lane < 64

        row = lax.broadcasted_iota(jnp.int32, (8, 128), 0)

        def finish(at):
            here = rows8(at)
            v = [flow.settled(sv0, c, at) for c in range(NCH)]
            if opening:
                ready = (row + at >= HALO + SUB) & (row + at < ROWS - HALO - SUB)
                for c in range(MAIN):
                    v[c] = jnp.where(ready, done[c, here, :], v[c])
            for h in range(2):
                total = v[h * R]
                for b in range(1, R):
                    total = total + v[h * R + b]
                sums[h, here, :] = total - float(R)
            sums[2, here, :] = v[MAIN] - 1.0
            sums[3, here, :] = v[MAIN + 1] - 1.0
            if step % 2:
                strip = jnp.where(near_left, v[MAIN + 1], v[MAIN])
                if not closing:
                    inner = gathered(v[:R], v[R:MAIN], column)
                for b in range(R):
                    place = R * lane + b
                    index = jnp.where(near_left, place + 64, place - (128 * R - 64))
                    got = picked(strip, jnp.clip(index, 0, 127))
                    v[b] = jnp.where(place < 2 * SUB, got, v[b])
                    v[R + b] = jnp.where(index >= 64 - 2 * SUB, jnp.where(near_left, v[R + b], got), v[R + b])
                if not closing:
                    v[MAIN] = jnp.where(lane >= 64 + 2 * SUB, inner, v[MAIN])
                    v[MAIN + 1] = jnp.where(lane < 64 - 2 * SUB, inner, v[MAIN + 1])
            if closing:
                for c in range(MAIN):
                    acc[c, here, :] = 0.45 * (v[c] - 1.0)
            else:
                for c in range(NCH):
                    new[c, here, :] = 0.9 * v[c] + 0.1

        def two(t):
            for u in range(2):
                finish(16 * t + 8 * start + 8 * u)

        loop(TILES // 2 - start, two)
        scale = 0.1 / (2.0 * R * R)
        pooled = []
        for at, n, fine in BANDS[: 1 if closing else 3]:
            parts = []
            for i in range(4):
                total = sums[i, pl.ds(fine, n, stride=R), :]
                for a in range(1, R):
                    total = total + sums[i, pl.ds(fine + a, n, stride=R), :]
                parts.append(total * scale)
            pooled.append(parts)
        if not closing:
            for i in range(4):
                rain[i, 0:16, :] = pooled[0][i]
                rain[i, 16:20, :] = pooled[1][i]
                rain[i, 20:24, :] = pooled[2][i]
        for t in range(2 if closing else 3):
            rows = slice(8 * t, 8 * t + 8)
            if closing:
                h0, h1, west, east = (pooled[0][i][rows] for i in range(4))
            else:
                h0, h1, west, east = (rain[i, rows, :] for i in range(4))
            west, east = strip_flux(west, east)
            h0 = jnp.where(lane < 3, west, h0)
            h1 = jnp.where(lane >= 125, east, h1)
            if closing:
                field[rows, 0:128] = h0
                field[rows, 128:256] = h1
            else:
                field[rows, :] = h0
                field[24 + 8 * t : 32 + 8 * t, :] = h1
                field[48 + 8 * t : 56 + 8 * t, :] = jnp.where(lane < 64, east, west)
        if closing:

            def lay(a):
                for b in range(R):
                    for h in range(2):
                        out[a * R + b, :, 128 * h : 128 * h + 128] = acc[h * R + b, pl.ds(HALO + a, NX, stride=R), :]

            loop(R, lay)


def call(kernel, args, out, scratch=(), hbm=False, limit=20, flops=0):
    return pl.pallas_call(
        kernel,
        out_shape=[jax.ShapeDtypeStruct(s, F32) for s in out],
        in_specs=[pl.BlockSpec(memory_space=pltpu.HBM if hbm else pltpu.VMEM)] * len(args),
        out_specs=[pl.BlockSpec(memory_space=pltpu.VMEM)] * len(out),
        scratch_shapes=[pltpu.VMEM(x, F32) if isinstance(x, tuple) else x for x in scratch],
        compiler_params=pltpu.CompilerParams(vmem_limit_bytes=limit * MIB),
        cost_estimate=pl.CostEstimate(flops=flops, bytes_accessed=5 * MIB, transcendentals=0) if flops else None,
    )(*args)


def pairs(axis, odd):
    n = lax.axis_size(axis)
    found = [(i, i + 1) for i in range(odd, n - 1, 2)]
    return found + [(j, i) for i, j in found]


def on_device(domain_state, coupling_field, regime, land_class, flow_code):
    tile = (2 * LEVELS, NX, NY)
    full, water, air = (MAIN, ROWS, 128), (NCH, ROWS, 128), (CH, 72, 128)
    strips, rim, small = (4, ROWS, 128), (384, 128), (72, 128)
    flows, inner_flows = (NCH, SVR, 128), (MAIN, SVR, 128)
    args = (domain_state[0], coupling_field[0], regime, land_class, flow_code)
    held = (
        tile,
        (NX, NY),
        pltpu.VMEM((NX, NY), jnp.int32),
        pltpu.VMEM(tile, jnp.int32),
        pltpu.VMEM(tile, jnp.int32),
        pltpu.SemaphoreType.DMA((3, R)),
        pltpu.SemaphoreType.DMA((2,)),
    )
    pay_a, pay_b = call(
        prep_kernel, args, ((3 * EDGE, 128), (3 * EDGE, 128)), held + ((3 * MAIN, OWN, 128),), hbm=True, limit=56
    )
    from_a = lax.ppermute(pay_a, "gx", pairs("gx", 0))
    from_b = lax.ppermute(pay_b, "gx", pairs("gx", 1))
    stw, sta, r02, r13, done = call(
        early_kernel,
        args,
        (full, air, full, full, full),
        held + (full, inner_flows, inner_flows),
        hbm=True,
        limit=26,
        flops=200_000_000,
    )
    stw, sta, r02, r13, sr, pay_c, pay_d = call(
        assemble_kernel, (stw, sta, r02, r13, from_a, from_b), (water, air, full, full, strips, rim, rim)
    )
    from_c = lax.ppermute(pay_c, "gy", pairs("gy", 0))
    from_d = lax.ppermute(pay_d, "gy", pairs("gy", 1))
    scratch = (water, flows, flows, (4, ROWS, 128), (4, ROWS, 128))
    for step in range(STEPS):
        kernel = functools.partial(route_kernel, step)
        if step == 0:
            stw, sta, sr, field = call(
                kernel,
                (stw, sta, r02, r13, sr, done, from_c, from_d),
                (water, air, strips, small),
                scratch + ((128, 24, 128),),
            )
        elif step < STEPS - 1:
            stw, sta, field = call(
                kernel, (stw, sta, r02, r13, sr, field), (water, air, small), scratch
            )
        else:
            out, field = call(
                kernel, (stw, sta, r02, r13, sr, field), (tile, (NX, NY)), scratch
            )
        field = lax.ppermute(field, "group", [(0, 1), (1, 0)])
    return (out[None], field[None])


def solution(mesh):
    return jax.shard_map(
        on_device,
        mesh=mesh,
        in_specs=(
            P("group", None, "gx", "gy"),
            P("group", "gx", "gy"),
            P("gx", "gy"),
            P(None, "gx", "gy"),
            P(None, "gx", "gy"),
        ),
        out_specs=(P("group", None, "gx", "gy"), P("group", "gx", "gy")),
        check_vma=False,
    )
```

```python
import functools
import math

import jax
import jax.numpy as jnp
from jax import lax
from jax.experimental import pallas as pl
from jax.experimental.pallas import tpu as pltpu
from jax.sharding import PartitionSpec as P

F32 = jnp.float32
R = 10
LEVELS = 50
STEPS = 4
SUB = 12
NX, NY = 16, 256
HALO = STEPS * SUB
OWN = NX * R
ROWS = OWN + 2 * HALO
TILES = ROWS // 8
MAIN = 2 * R
NCH = MAIN + 2
SVR = ROWS + 16
EDGE = MAIN * HALO
CH = 2 * LEVELS + 2
RANGES = (
    ((0, 8, 12),),
    ((1, 10, 4), (2, 14, 8)),
    ((3, 13, 8), (4, 8, 4)),
    ((4, 8, 4), (5, 11, 8)),
)
MIB = 1024 * 1024
EDGE_TILES = 9


def rows8(start):
    return pl.ds(start if isinstance(start, int) else pl.multiple_of(start, 8), 8)


def lanes():
    return lax.broadcasted_iota(jnp.int32, (8, 128), 1)


def picked(x, index):
    return jnp.take_along_axis(x, index, axis=1, mode="promise_in_bounds")


def loop(n, body):
    def step(i, carry):
        body(i)
        return carry

    lax.fori_loop(0, n, step, 0)


def info_of():
    return [lax.axis_index(a) for a in ("group", "gx", "gy")]


class Inputs:
    def __init__(self, hbm, vmem, sems, sems2):
        self.dom, self.coup, self.regime, self.land, self.flow = vmem
        self.big = [(hbm[i], vmem[i]) for i in (0, 3, 4)]
        self.small = [pltpu.make_async_copy(hbm[i], vmem[i], sems2.at[i - 1]) for i in (1, 2)]
        self.sems = sems

    def part(self, k, i):
        src, dst = self.big[k]
        cut = pl.ds(i * R, R)
        return pltpu.make_async_copy(src.at[cut], dst.at[cut], self.sems.at[k, i])

    def start(self, kinds):
        for x in self.small:
            x.start(priority=1)
        for i in range(R):
            for k in range(kinds):
                self.part(k, i).start(priority=1)
        for x in self.small:
            x.wait()

    def wait(self, kinds, i):
        for k in range(kinds):
            self.part(k, i).wait()

    def lay_out(self, put):
        self.start(3)

        def one(a):
            self.wait(3, a)
            for b in range(R):
                c = a * R + b
                for h in range(2):
                    cols = slice(128 * h, 128 * h + 128)
                    land_value = self.land[c, :, cols].astype(F32)
                    code = self.flow[c, :, cols]
                    rate = 0.3 + 0.08 * land_value
                    keep = 1.0 - (0.6 - 0.07 * land_value)
                    water = self.dom[c, :, cols] + keep * self.coup[:, cols]
                    put(0, h * R + b, a, 2.0 * water + 1.0)
                    put(1, h * R + b, a, jnp.where(code == 0, rate, jnp.where(code == 2, -rate, 0.0)))
                    put(2, h * R + b, a, jnp.where(code == 1, rate, jnp.where(code == 3, -rate, 0.0)))

        loop(R, one)

    def blocks(self, put):
        self.start(1)

        def one(i):
            self.wait(1, i)
            for u in range(10):
                for h in range(2):
                    for t in range(2):
                        put(i * 10 + u, h, t, self.dom[i * 10 + u, 8 * t : 8 * t + 8, 128 * h : 128 * h + 128])

        loop(R, one)
        for h in range(2):
            for t in range(2):
                cut = (slice(8 * t, 8 * t + 8), slice(128 * h, 128 * h + 128))
                put(100, h, t, self.coup[cut])
                put(101, h, t, self.regime[cut].astype(F32))


def prep_kernel(*refs):
    pay_a, pay_b, own, sems = refs[14:]
    inputs = Inputs(refs[:5], refs[7:12], *refs[12:14])

    def sent(i, start, n):
        part = pl.ds(start, n)
        return pltpu.make_async_copy((pay_a, pay_b)[i].at[part], refs[5 + i].at[part], sems.at[i, start // EDGE])

    group, gx, _ = info_of()
    even = lax.rem(gx, 2) == 0

    @pl.when(group == 1)
    def _():
        def put(k, c, a, value):
            own[k * MAIN + c, pl.ds(a, NX, stride=R), :] = value

        inputs.lay_out(put)
        low = jnp.where(even, OWN - HALO, 0)

        def rim(i):
            for t in range(HALO // 8):
                pay_a[rows8(i * HALO + 8 * t), :] = own[i, rows8(low + 8 * t), :]
                pay_b[rows8(i * HALO + 8 * t), :] = own[i, rows8(OWN - HALO - low + 8 * t), :]

        copies = []
        for k in range(3):
            loop(MAIN, lambda c: rim(k * MAIN + c))
            copies += [sent(i, k * EDGE, EDGE) for i in range(2)]
            for x in copies[-2:]:
                x.start()
        for x in copies:
            x.wait()

    @pl.when(group == 0)
    def _():
        def put(c, h, t, value):
            @pl.when(even == (t == 1))
            def _():
                pay_a[rows8((c * 2 + h) * 8), :] = value

            @pl.when(even == (t == 0))
            def _():
                pay_b[rows8((c * 2 + h) * 8), :] = value

        inputs.blocks(put)
        copies = [sent(i, 0, CH * 16) for i in range(2)]
        for x in copies:
            x.start()
        for x in copies:
            x.wait()


def early_kernel(*refs):
    stw, sta, r02, r13, inner = refs[5:10]
    inputs = Inputs(refs[:5], refs[10:15], *refs[15:17])
    acc, sv0, sv1 = refs[17:]
    group, _, _ = info_of()

    @pl.when(group == 1)
    def _():
        def put(k, c, a, value):
            (stw, r02, r13)[k][c, pl.ds(HALO + a, NX, stride=R), :] = value

        inputs.lay_out(put)
        begin = HALO // 8

        def fill(t):
            here = rows8(8 * (t + begin))
            for c in range(MAIN):
                acc[c, here, :] = stw[c, here, :]

        loop(OWN // 8, fill)
        zero = jnp.zeros((8, 128), F32)

        def clear(t):
            for c in range(MAIN):
                sv0[c, rows8(8 * (t + begin)), :] = zero

        loop(OWN // 8 + 2, clear)
        for c in range(MAIN):
            sv1[c, rows8(8 * begin), :] = zero
            sv1[c, rows8(HALO + OWN + 8), :] = zero
        flow = Flow(acc, lambda k, c, here: (r02, r13)[k][c, here, :])

        for trim, substeps in ((0, 8), (1, 4)):

            def pair(_):
                size = OWN // 16 - trim
                for sv in ((sv0, sv1), (sv1, sv0)):
                    loop(2, functools.partial(flow.substep, begin + trim, size, *sv, range(2), ()))

            loop(substeps // 2, pair)

        def finish(t):
            for u in range(2):
                at = 16 * t + HALO + 8 + 8 * u
                for c in range(MAIN):
                    inner[c, rows8(at), :] = flow.settled(sv0, c, at)

        loop(OWN // 16 - 1, finish)

    @pl.when(group == 0)
    def _():
        def put(c, h, t, value):
            sta[c, 24 * h + 8 * t : 24 * h + 8 * t + 8, :] = value

        inputs.blocks(put)


class Flow:
    def __init__(self, acc, rate):
        self.acc, self.rate = acc, rate

    def settled(self, sv, c, at):
        above = jnp.maximum(sv[c, pl.ds(at + 7, 8), :], 0.0)
        below = jnp.minimum(sv[c, pl.ds(at + 9, 8), :], 0.0)
        return self.acc[c, rows8(at), :] + above - below

    def substep(self, begin, group, sv_in, sv_out, halves, strips, i):
        acc, lane = self.acc, lanes()
        start = pl.multiple_of(i * (8 * group), 8) + 8 * begin
        for g in range(group):
            at = start + 8 * g
            here = rows8(at)

            def cell(c):
                v = self.settled(sv_in, c, at)
                q = (v - 2.0) + pltpu.reciprocal(v, approx=True)
                down, across = self.rate(1, c, here) * q, self.rate(0, c, here) * q
                sv_out[c, rows8(at + 8), :] = down
                return v - jnp.abs(down + across), across

            heads = [cell(h * R) for h in halves]
            tails = [cell(h * R + R - 1) for h in halves]
            east = [pltpu.roll(jnp.maximum(x[1], 0.0), 1, 1) for x in tails]
            west = [pltpu.roll(jnp.minimum(x[1], 0.0), 127, 1) for x in heads]
            for c in strips:
                kept, across = cell(c)
                kept = kept + pltpu.roll(jnp.maximum(across, 0.0), 1, 1)
                acc[c, here, :] = kept - pltpu.roll(jnp.minimum(across, 0.0), 127, 1)
            for h in halves:
                this = heads[h]
                value = this[0] + jnp.where(lane == 0, east[1 - h], east[h])
                for b in range(1, R):
                    after = cell(h * R + b) if b < R - 1 else tails[h]
                    acc[h * R + b - 1, here, :] = value - jnp.minimum(after[1], 0.0)
                    value = after[0] + jnp.maximum(this[1], 0.0)
                    this = after
                acc[h * R + R - 1, here, :] = value - jnp.where(lane == 127, west[1 - h], west[h])


def strip_map():
    lane = lanes()
    fine = jnp.where(lane >= 64, lane - 64, lane + (NY * R - 64))
    return fine % R, fine // R % 128


def gathered(left, right, column):
    b_of, y_of = column
    near_left = lanes() < 64
    out = None
    for b in range(R):
        found = picked(jnp.where(near_left, left[b], right[b]), y_of)
        out = found if b == 0 else jnp.where(b_of == b, found, out)
    return out


def assemble_kernel(stw_in, sta_in, r02_in, r13_in, from_a, from_b, stw, sta, r02, r13, sr, pay_c, pay_d):
    group, gx, gy = info_of()
    even_x, even_y = lax.rem(gx, 2) == 0, lax.rem(gy, 2) == 0
    lane = lanes()

    @pl.when(group == 1)
    def _():
        at_a = jnp.where(even_x, ROWS - HALO, 0)
        at_b = ROWS - HALO - at_a

        def one(c):
            def join(v, h, w, to):
                stw[c, to, :] = v
                r02[c, to, :] = h
                r13[c, to, :] = w

            for t in range(OWN // 8):
                here = rows8(HALO + 8 * t)
                join(stw_in[c, here, :], r02_in[c, here, :], r13_in[c, here, :], here)
            for src, at in ((from_a, at_a), (from_b, at_b)):
                for t in range(HALO // 8):
                    v, h, w = (src[rows8((k * MAIN + c) * HALO + 8 * t), :] for k in range(3))
                    join(jnp.where(v == 0.0, 1.0, v), h, w, rows8(at + 8 * t))

        loop(MAIN, one)
        column = strip_map()

        def strips(t):
            for k, src in enumerate((stw, r02, r13)):
                found = []
                for half in range(2):
                    here = rows8(8 * t + 128 * half)
                    got = gathered([src[b, here, :] for b in range(R)], [src[R + b, here, :] for b in range(R)], column)
                    found.append(got)
                    if k == 0:
                        stw[MAIN, here, :] = got
                    else:
                        sr[2 * k - 2, here, :] = got
                one, two = found
                turned = pltpu.roll(two, 64, 1)
                to_left = jnp.where(lane >= 64, one, turned)
                to_right = jnp.where(lane < 64, one, turned)
                pay_c[rows8(k * 128 + 8 * t), :] = jnp.where(even_y, to_right, to_left)
                pay_d[rows8(k * 128 + 8 * t), :] = jnp.where(even_y, to_left, to_right)

        loop(16, strips)

    @pl.when(group == 0)
    def _():
        sub = lax.broadcasted_iota(jnp.int32, (8, 128), 0)

        def one(c):
            for h in range(2):
                for t in range(2):
                    here = slice(24 * h + 8 * t, 24 * h + 8 * t + 8)
                    sta[c, here, :] = sta_in[c, here, :]
                a, b = (x[rows8((c * 2 + h) * 8), :] for x in (from_a, from_b))
                above, below = jnp.where(even_x, b, a), jnp.where(even_x, a, b)
                sta[c, 24 * h + 16 : 24 * h + 24, :] = jnp.where(sub >= 4, above, below)

        loop(CH, one)

        def pack(i):
            k, t = i // 3, lax.rem(i, 3)
            to_left = jnp.zeros((8, 128), F32)
            to_right = to_left
            for j in range(32):
                c = jnp.minimum(32 * k + j, CH - 1)
                here = (lane >= 4 * j) & (lane < 4 * j + 4)
                west = sta[c, rows8(8 * t), :]
                east = sta[c, rows8(24 + 8 * t), :]
                to_left = jnp.where(here, pltpu.roll(west, 4 * j, 1), to_left)
                to_right = jnp.where(here, pltpu.roll(east, (4 * j + 4) % 128, 1), to_right)
            pay_c[rows8(k * 24 + 8 * t), :] = jnp.where(even_y, to_right, to_left)
            pay_d[rows8(k * 24 + 8 * t), :] = jnp.where(even_y, to_left, to_right)

        loop(12, pack)


def atmosphere_column(load, flux, regime, put):
    mixing = jnp.where(regime == 2.0, 0.4, 0.05)
    efficiency = jnp.where(regime == 0.0, 0.3, jnp.where(regime == 1.0, 0.6, 0.9))
    heat, damp = load(0) + flux, load(LEVELS) + flux
    heat_below, damp_below = heat, damp
    total = jnp.zeros((8, 128), F32)
    for k in range(LEVELS):
        last = k == LEVELS - 1
        heat_above = heat if last else load(k + 1)
        damp_above = damp if last else load(LEVELS + k + 1)
        t = heat + mixing * (heat_above + heat_below - 2.0 * heat)
        m = damp + mixing * (damp_above + damp_below - 2.0 * damp)
        capacity = (0.8 * math.exp(-3.0 * k / LEVELS)) * jnp.exp(0.3 * t)
        formed = efficiency * jnp.maximum(m - capacity, 0.0)
        put(k, t + 0.5 * formed)
        put(LEVELS + k, m - formed)
        total = total + formed
        heat_below, damp_below, heat, damp = heat, damp, heat_above, damp_above
    return total * (2.0 / LEVELS)


BANDS = ((0, 16, HALO), (16, 4, HALO + OWN), (20, 4, HALO - 4 * R))


def strip_rain(h0, h1, side, t):
    lane = lanes()
    here = slice(8 * t, 8 * t + 8)
    y = (lane + 16) // R - 8
    left = jnp.where(
        y < 0, picked(side[here], jnp.clip(128 + y, 0, 127)), picked(h0[here], jnp.clip(y, 0, 127))
    )
    y = (lane + (NY * R - 64)) // R
    right = jnp.where(
        y < NY, picked(h1[here], jnp.clip(y - 128, 0, 127)), picked(side[here], jnp.clip(y - NY, 0, 127))
    )
    return left, right


def strip_flux(left, right):
    lane = lanes()
    out = []
    for x, start in (
        (left, jnp.where(lane < 64, 64 + R * lane, 64 + R * (lane - 128))),
        (right, jnp.where(lane < 64, 64 + R * lane, 64 + R * (lane - 128))),
    ):
        back = lambda v, n: pltpu.roll(v, 128 - n, 1)
        two = x + back(x, 1)
        four = two + back(two, 2)
        ten = four + back(four, 4) + back(two, 8)
        out.append(picked(ten, jnp.clip(start, 0, 127)))
    return out


def route_kernel(step, *refs):
    opening, closing, merging = step == 0, step == STEPS - 1, step % 2 == 1
    if opening:
        stw, sta, r02, r13, sr_in, done, from_c, from_d, new, new_a, field, sr = refs[:12]
        acc, sv0, sv1, rain, sums, side_a = refs[12:]
        fld = None
    elif merging:
        stw, sta, r02, r13, sr, fld, acc, sv0, new_a, field = refs[:10]
        sv1, rain, sums = refs[10:]
    else:
        stw, sta, r02, r13, sr, fld, new, new_a, field = refs[:9]
        acc, sv0, sv1, rain, sums = refs[9:]
    group, _, gy = info_of()
    even_y = lax.rem(gy, 2) == 0
    lane = lanes()
    ranges = RANGES[step]
    first = ranges[0][0]
    count = TILES - 2 * first

    @pl.when(group == 0)
    def _():
        if opening:

            def side(i):
                k, t = i // 3, lax.rem(i, 3)
                c, d = from_c[rows8(k * 24 + 8 * t), :], from_d[rows8(k * 24 + 8 * t), :]
                west, east = jnp.where(even_y, d, c), jnp.where(even_y, c, d)
                for j in range(32):
                    side_a[32 * k + j, rows8(8 * t), :] = jnp.where(
                        lane < 4,
                        pltpu.roll(east, (128 - 4 * j) % 128, 1),
                        jnp.where(lane >= 124, pltpu.roll(west, 124 - 4 * j, 1), 0.0),
                    )

            loop(12, side)

        if closing:

            def own(i):
                h, t = i // 2, lax.rem(i, 2)
                here = rows8(24 * h + 8 * t)

                def put(c, value):
                    new_a[c, here, :] = value

                total = atmosphere_column(lambda c: sta[c, here, :], fld[here, :], sta[CH - 1, here, :], put)
                for u in range(2):

                    @pl.when(h == u)
                    def _():
                        field[rows8(8 * t), 128 * u : 128 * u + 128] = total

            loop(4, own)
        else:

            def block(load, here):
                def put(c, value):
                    new_a[c, here, :] = value

                regime = load(CH - 1)
                put(CH - 1, regime)
                flux = load(CH - 2) if opening else fld[here, :]
                field[here, :] = atmosphere_column(load, flux, regime, put)

            def inner(i):
                here = rows8(8 * i)
                block(lambda c: sta[c, here, :], here)

            def outer(t):
                block(lambda c: side_a[c, rows8(8 * t), :], rows8(48 + 8 * t))

            if opening:
                loop(6, inner)
                loop(3, outer)
            else:
                loop(9, inner)

    @pl.when(group == 1)
    def _():
        zero = jnp.zeros((8, 128), F32)
        if opening:

            def side(t):
                for half in range(2):
                    here = rows8(8 * t + 128 * half)
                    for k in range(3):
                        c, d = from_c[rows8(k * 128 + 8 * t), :], from_d[rows8(k * 128 + 8 * t), :]
                        west, east = jnp.where(even_y, d, c), jnp.where(even_y, c, d)
                        if half:
                            west, east = pltpu.roll(west, 64, 1), pltpu.roll(east, 64, 1)
                        if k == 0:
                            west = jnp.where(west == 0.0, 1.0, west)
                            east = jnp.where(east == 0.0, 1.0, east)
                        inner = sr_in[2 * k - 2, here, :] if k else stw[MAIN, here, :]
                        left = jnp.where(lane >= 64, inner, west)
                        right = jnp.where(lane < 64, inner, east)
                        if k == 0:
                            acc[MAIN, here, :] = left
                            acc[MAIN + 1, here, :] = right
                        else:
                            sr[2 * k - 2, here, :] = left
                            sr[2 * k - 1, here, :] = right

            loop(16, side)

        def of(main, k, c, here):
            return main[c, here, :] if c < MAIN else sr[2 * k + c - MAIN, here, :]

        if opening:

            def fill(t):
                for at in (8 * t, 8 * t + 8 * (TILES - EDGE_TILES)):
                    for c in range(MAIN):
                        acc[c, rows8(at), :] = stw[c, rows8(at), :]

        else:
            blocks = [fld[pl.ds(24 * i, 24), :] for i in range(3)]
            found = [strip_rain(*blocks, t) for t in range(3)]
            for at, n, fine in BANDS:
                if n == 16:
                    pieces = [b[:16] for b in blocks[:2]]
                    pieces += [jnp.concatenate([found[0][i], found[1][i]], 0) for i in range(2)]
                else:
                    cut = slice(at - 16, at - 12)
                    pieces = [b[at : at + 4] for b in blocks[:2]] + [found[2][i][cut] for i in range(2)]
                for i, piece in enumerate(pieces):
                    for a in range(R):
                        rain[i, pl.ds(fine + a, n, stride=R), :] = piece

            def fill(t):
                here = rows8(8 * (t + first))
                for c in range(NCH):
                    fall = rain[c // R if c < MAIN else c - MAIN + 2, here, :]
                    rate = jnp.abs(of(r02, 0, c, here) + of(r13, 1, c, here))
                    share = 0.275 + 1.75 * rate
                    acc[c, here, :] = stw[c, here, :] + share * fall

        loop(EDGE_TILES if opening else count, fill)

        def clear(t):
            for c in range(NCH):
                sv0[c, rows8(8 * (t + first)), :] = zero

        loop(count + 2, clear)
        for c in range(NCH):
            sv1[c, rows8(8 * first), :] = zero
            sv1[c, rows8(8 * (first + count + 1)), :] = zero

        flow = Flow(acc, lambda k, c, here: of((r02, r13)[k], k, c, here))
        strips = (MAIN, MAIN + 1)
        if opening:
            for c in range(MAIN):
                sv1[c, rows8(8 * (EDGE_TILES + 1)), :] = zero
                sv1[c, rows8(8 * (TILES - EDGE_TILES)), :] = zero

            for trim, substeps in ((0, 8), (1, 4)):

                def pair(_):
                    size = EDGE_TILES - 2 * trim
                    for sv in ((sv0, sv1), (sv1, sv0)):
                        flow.substep(trim, size, *sv, range(2), (), 0)
                        flow.substep(TILES - trim - size, size, *sv, range(2), (), 0)
                        loop(2, functools.partial(flow.substep, 0, TILES // 2, *sv, (), strips))

                loop(substeps // 2, pair)
        else:
            for begin, size, substeps in ranges:

                def pair(_):
                    times = (TILES - 2 * begin) // size
                    loop(times, functools.partial(flow.substep, begin, size, sv0, sv1, range(2), strips))
                    loop(times, functools.partial(flow.substep, begin, size, sv1, sv0, range(2), strips))

                loop(substeps // 2, pair)

        start = HALO // 8 if closing else RANGES[step + 1][0][0]

        def tally(at):
            here = rows8(at)
            for h in range(2):
                total = None
                for c in range(h * R, h * R + R):
                    v = flow.settled(sv0, c, at)
                    if opening:
                        v = jnp.where(early_rows(at), done[c, here, :], v)
                    if not merging:
                        new[c, here, :] = 0.9 * v + 0.1
                    total = v if total is None else total + v
                sums[h, here, :] = total - float(R)
            for c in (MAIN, MAIN + 1):
                v = flow.settled(sv0, c, at)
                if not merging:
                    new[c, here, :] = 0.9 * v + 0.1
                sums[c - MAIN + 2, here, :] = v - 1.0

        def two(t):
            for u in range(2):
                tally(16 * t + 8 * start + 8 * u)

        loop(TILES // 2 - start, two)
        scale = 0.1 / (2.0 * R * R)
        pooled = []
        for at, n, fine in BANDS[: 1 if closing else 3]:
            parts = []
            for i in range(4):
                total = sums[i, pl.ds(fine, n, stride=R), :]
                for a in range(1, R):
                    total = total + sums[i, pl.ds(fine + a, n, stride=R), :]
                parts.append(total * scale)
            pooled.append(parts)
        if not closing:
            for i in range(4):
                rain[i, 0:16, :] = pooled[0][i]
                rain[i, 16:20, :] = pooled[1][i]
                rain[i, 20:24, :] = pooled[2][i]
        for t in range(2 if closing else 3):
            rows = slice(8 * t, 8 * t + 8)
            if closing:
                h0, h1, west, east = (pooled[0][i][rows] for i in range(4))
            else:
                h0, h1, west, east = (rain[i, rows, :] for i in range(4))
            west, east = strip_flux(west, east)
            h0 = jnp.where(lane < 3, west, h0)
            h1 = jnp.where(lane >= 125, east, h1)
            if closing:
                field[rows, 0:128] = h0
                field[rows, 128:256] = h1
            else:
                field[rows, :] = h0
                field[24 + 8 * t : 32 + 8 * t, :] = h1
                field[48 + 8 * t : 56 + 8 * t, :] = jnp.where(lane < 64, east, west)


def early_rows(at):
    row = lax.broadcasted_iota(jnp.int32, (8, 128), 0) + at
    return (row >= HALO + SUB) & (row < ROWS - HALO - SUB)


def settle_kernel(step, *refs):
    closing = step == STEPS - 1
    if closing:
        acc, sv0, sta, out, last = refs
    else:
        acc, sv0, new = refs
    group, _, _ = info_of()
    lane = lanes()

    @pl.when(group == 1)
    def _():
        flow = Flow(acc, None)
        column = strip_map()
        start = HALO // 8 if closing else RANGES[step + 1][0][0]
        near_left = lane < 64

        def finish(at):
            here = rows8(at)
            v = [flow.settled(sv0, c, at) for c in range(NCH)]
            strip = jnp.where(near_left, v[MAIN + 1], v[MAIN])
            if not closing:
                inner = gathered(v[:R], v[R:MAIN], column)
            for b in range(R):
                place = R * lane + b
                index = jnp.where(near_left, place + 64, place - (128 * R - 64))
                got = picked(strip, jnp.clip(index, 0, 127))
                v[b] = jnp.where(place < 2 * SUB, got, v[b])
                v[R + b] = jnp.where(index >= 64 - 2 * SUB, jnp.where(near_left, v[R + b], got), v[R + b])
            if not closing:
                v[MAIN] = jnp.where(lane >= 64 + 2 * SUB, inner, v[MAIN])
                v[MAIN + 1] = jnp.where(lane < 64 - 2 * SUB, inner, v[MAIN + 1])
            if closing:
                for c in range(MAIN):
                    last[c, rows8(at - HALO), :] = 0.45 * (v[c] - 1.0)
            else:
                for c in range(NCH):
                    new[c, here, :] = 0.9 * v[c] + 0.1

        def two(t):
            for u in range(2):
                finish(16 * t + 8 * start + 8 * u)

        loop(TILES // 2 - start, two)
        if closing:

            def lay(a):
                for b in range(R):
                    for h in range(2):
                        out[a * R + b, :, 128 * h : 128 * h + 128] = last[h * R + b, pl.ds(a, NX, stride=R), :]

            loop(R, lay)

    if closing:

        @pl.when(group == 0)
        def _():
            def copy(i):
                for u in range(10):
                    for h in range(2):
                        out[i * 10 + u, :, 128 * h : 128 * h + 128] = sta[i * 10 + u, 24 * h : 24 * h + 16, :]

            loop(R, copy)


def call(kernel, args, out, scratch=(), hbm=False, out_hbm=False, limit=16, flops=0):
    return pl.pallas_call(
        kernel,
        out_shape=[jax.ShapeDtypeStruct(s, F32) for s in out],
        in_specs=[pl.BlockSpec(memory_space=pltpu.HBM if hbm else pltpu.VMEM)] * len(args),
        out_specs=[pl.BlockSpec(memory_space=pltpu.HBM if out_hbm else pltpu.VMEM)] * len(out),
        scratch_shapes=[pltpu.VMEM(x, F32) if isinstance(x, tuple) else x for x in scratch],
        compiler_params=pltpu.CompilerParams(vmem_limit_bytes=limit * MIB),
        cost_estimate=pl.CostEstimate(flops=flops, bytes_accessed=5 * MIB, transcendentals=0) if flops else None,
    )(*args)


def pairs(axis, odd):
    n = lax.axis_size(axis)
    found = [(i, i + 1) for i in range(odd, n - 1, 2)]
    return found + [(j, i) for i, j in found]


def on_device(domain_state, coupling_field, regime, land_class, flow_code):
    tile = (2 * LEVELS, NX, NY)
    full, water, air = (MAIN, ROWS, 128), (NCH, ROWS, 128), (CH, 72, 128)
    strips, rim, small = (4, ROWS, 128), (384, 128), (72, 128)
    flows, inner_flows = (NCH, SVR, 128), (MAIN, SVR, 128)
    args = (domain_state[0], coupling_field[0], regime, land_class, flow_code)
    held = (
        tile,
        (NX, NY),
        pltpu.VMEM((NX, NY), jnp.int32),
        pltpu.VMEM(tile, jnp.int32),
        pltpu.VMEM(tile, jnp.int32),
        pltpu.SemaphoreType.DMA((3, R)),
        pltpu.SemaphoreType.DMA((2,)),
    )
    edge = (3 * EDGE, 128)
    pay_a, pay_b = call(
        prep_kernel,
        args,
        (edge, edge),
        held + (edge, edge, (3 * MAIN, OWN, 128), pltpu.SemaphoreType.DMA((2, 3))),
        hbm=True,
        out_hbm=True,
        limit=56,
    )
    from_a = lax.ppermute(pay_a, "gx", pairs("gx", 0))
    from_b = lax.ppermute(pay_b, "gx", pairs("gx", 1))
    stw, sta, r02, r13, done = call(
        early_kernel,
        args,
        (full, air, full, full, full),
        held + (full, inner_flows, inner_flows),
        hbm=True,
        limit=17,
        flops=200_000_000,
    )
    stw, sta, r02, r13, sr, pay_c, pay_d = call(
        assemble_kernel, (stw, sta, r02, r13, from_a, from_b), (water, air, full, full, strips, rim, rim)
    )
    from_c = lax.ppermute(pay_c, "gy", pairs("gy", 0))
    from_d = lax.ppermute(pay_d, "gy", pairs("gy", 1))
    spare = (flows, (4, ROWS, 128), (4, ROWS, 128))
    scratch = (water, flows) + spare
    for step in range(STEPS):
        kernel = functools.partial(route_kernel, step)
        settle = functools.partial(settle_kernel, step)
        if step == 0:
            stw, sta, field, sr = call(
                kernel,
                (stw, sta, r02, r13, sr, done, from_c, from_d),
                (water, air, small, strips),
                scratch + ((128, 24, 128),),
            )
        elif step % 2 == 0:
            stw, sta, field = call(kernel, (stw, sta, r02, r13, sr, field), (water, air, small), scratch)
        else:
            shape = (NX, NY) if step == STEPS - 1 else small
            acc, sv, sta, field = call(
                kernel, (stw, sta, r02, r13, sr, field), (water, flows, air, shape), spare
            )
        field = lax.ppermute(field, "group", [(0, 1), (1, 0)])
        if step == STEPS - 1:
            out = call(settle, (acc, sv, sta), (tile,), ((MAIN, OWN, 128),), flops=50_000_000)[0]
        elif step % 2:
            stw = call(settle, (acc, sv), (water,), flops=50_000_000)[0]
    return (out[None], field[None])


def solution(mesh):
    return jax.shard_map(
        on_device,
        mesh=mesh,
        in_specs=(
            P("group", None, "gx", "gy"),
            P("group", "gx", "gy"),
            P("gx", "gy"),
            P(None, "gx", "gy"),
            P(None, "gx", "gy"),
        ),
        out_specs=(P("group", None, "gx", "gy"), P("group", "gx", "gy")),
        check_vma=False,
    )
```

```python
import functools
import math

import jax
import jax.numpy as jnp
from jax import lax
from jax.experimental import pallas as pl
from jax.experimental.pallas import tpu as pltpu
from jax.sharding import PartitionSpec as P

F32 = jnp.float32
R = 10
LEVELS = 50
STEPS = 4
SUB = 12
NX, NY = 16, 256
HALO = STEPS * SUB
OWN = NX * R
ROWS = OWN + 2 * HALO
TILES = ROWS // 8
MAIN = 2 * R
NCH = MAIN + 2
SVR = ROWS + 16
EDGE = MAIN * HALO
CH = 2 * LEVELS + 2
RANGES = (
    ((0, 8, 12),),
    ((1, 10, 4), (2, 14, 8)),
    ((3, 13, 8), (4, 8, 4)),
    ((4, 8, 4), (5, 11, 8)),
)
MIB = 1024 * 1024
EDGE_TILES = 9


def rows8(start):
    return pl.ds(start if isinstance(start, int) else pl.multiple_of(start, 8), 8)


def lanes():
    return lax.broadcasted_iota(jnp.int32, (8, 128), 1)


def picked(x, index):
    return jnp.take_along_axis(x, index, axis=1, mode="promise_in_bounds")


def loop(n, body):
    def step(i, carry):
        body(i)
        return carry

    lax.fori_loop(0, n, step, 0)


def info_of():
    return [lax.axis_index(a) for a in ("group", "gx", "gy")]


class Inputs:
    def __init__(self, hbm, vmem, sems, sems2):
        self.dom, self.coup, self.regime, self.land, self.flow = vmem
        self.big = [(hbm[i], vmem[i]) for i in (0, 3, 4)]
        self.small = [pltpu.make_async_copy(hbm[i], vmem[i], sems2.at[i - 1]) for i in (1, 2)]
        self.sems = sems

    def part(self, k, i):
        src, dst = self.big[k]
        cut = pl.ds(i * R, R)
        return pltpu.make_async_copy(src.at[cut], dst.at[cut], self.sems.at[k, i])

    def start(self, kinds):
        for x in self.small:
            x.start(priority=1)
        for i in range(R):
            for k in range(kinds):
                self.part(k, i).start(priority=1)
        for x in self.small:
            x.wait()

    def wait(self, kinds, i):
        for k in range(kinds):
            self.part(k, i).wait()

    def lay_out(self, put):
        self.start(3)

        def one(a):
            self.wait(3, a)
            for b in range(R):
                c = a * R + b
                for h in range(2):
                    cols = slice(128 * h, 128 * h + 128)
                    land_value = self.land[c, :, cols].astype(F32)
                    code = self.flow[c, :, cols]
                    rate = 0.3 + 0.08 * land_value
                    keep = 1.0 - (0.6 - 0.07 * land_value)
                    water = self.dom[c, :, cols] + keep * self.coup[:, cols]
                    put(0, h * R + b, a, 2.0 * water + 1.0)
                    put(1, h * R + b, a, jnp.where(code == 0, rate, jnp.where(code == 2, -rate, 0.0)))
                    put(2, h * R + b, a, jnp.where(code == 1, rate, jnp.where(code == 3, -rate, 0.0)))

        loop(R, one)

    def blocks(self, put):
        self.start(1)

        def one(i):
            self.wait(1, i)
            for u in range(10):
                for h in range(2):
                    for t in range(2):
                        put(i * 10 + u, h, t, self.dom[i * 10 + u, 8 * t : 8 * t + 8, 128 * h : 128 * h + 128])

        loop(R, one)
        for h in range(2):
            for t in range(2):
                cut = (slice(8 * t, 8 * t + 8), slice(128 * h, 128 * h + 128))
                put(100, h, t, self.coup[cut])
                put(101, h, t, self.regime[cut].astype(F32))


def prep_kernel(*refs):
    pay_a, pay_b, own, sems = refs[14:]
    inputs = Inputs(refs[:5], refs[7:12], *refs[12:14])

    def sent(i, start, n):
        part = pl.ds(start, n)
        return pltpu.make_async_copy((pay_a, pay_b)[i].at[part], refs[5 + i].at[part], sems.at[i, start // EDGE])

    group, gx, _ = info_of()
    even = lax.rem(gx, 2) == 0

    @pl.when(group == 1)
    def _():
        def put(k, c, a, value):
            own[k * MAIN + c, pl.ds(a, NX, stride=R), :] = value

        inputs.lay_out(put)
        low = jnp.where(even, OWN - HALO, 0)

        def rim(i):
            for t in range(HALO // 8):
                pay_a[rows8(i * HALO + 8 * t), :] = own[i, rows8(low + 8 * t), :]
                pay_b[rows8(i * HALO + 8 * t), :] = own[i, rows8(OWN - HALO - low + 8 * t), :]

        copies = []
        for k in range(3):
            loop(MAIN, lambda c: rim(k * MAIN + c))
            copies += [sent(i, k * EDGE, EDGE) for i in range(2)]
            for x in copies[-2:]:
                x.start()
        for x in copies:
            x.wait()

    @pl.when(group == 0)
    def _():
        def put(c, h, t, value):
            @pl.when(even == (t == 1))
            def _():
                pay_a[rows8((c * 2 + h) * 8), :] = value

            @pl.when(even == (t == 0))
            def _():
                pay_b[rows8((c * 2 + h) * 8), :] = value

        inputs.blocks(put)
        copies = [sent(i, 0, CH * 16) for i in range(2)]
        for x in copies:
            x.start()
        for x in copies:
            x.wait()


def early_kernel(*refs):
    stw, sta, r02, r13, inner = refs[5:10]
    inputs = Inputs(refs[:5], refs[10:15], *refs[15:17])
    acc, sv0, sv1 = refs[17:]
    group, _, _ = info_of()

    @pl.when(group == 1)
    def _():
        def put(k, c, a, value):
            (stw, r02, r13)[k][c, pl.ds(HALO + a, NX, stride=R), :] = value

        inputs.lay_out(put)
        begin = HALO // 8

        def fill(t):
            here = rows8(8 * (t + begin))
            for c in range(MAIN):
                acc[c, here, :] = stw[c, here, :]

        loop(OWN // 8, fill)
        zero = jnp.zeros((8, 128), F32)

        def clear(t):
            for c in range(MAIN):
                sv0[c, rows8(8 * (t + begin)), :] = zero

        loop(OWN // 8 + 2, clear)
        for c in range(MAIN):
            sv1[c, rows8(8 * begin), :] = zero
            sv1[c, rows8(HALO + OWN + 8), :] = zero
        flow = Flow(acc, lambda k, c, here: (r02, r13)[k][c, here, :])

        for trim, substeps in ((0, 8), (1, 4)):

            def pair(_):
                size = OWN // 16 - trim
                for sv in ((sv0, sv1), (sv1, sv0)):
                    loop(2, functools.partial(flow.substep, begin + trim, size, *sv, range(2), ()))

            loop(substeps // 2, pair)

        def finish(t):
            for u in range(2):
                at = 16 * t + HALO + 8 + 8 * u
                for c in range(MAIN):
                    inner[c, rows8(at), :] = flow.settled(sv0, c, at)

        loop(OWN // 16 - 1, finish)

    @pl.when(group == 0)
    def _():
        def put(c, h, t, value):
            sta[c, 24 * h + 8 * t : 24 * h + 8 * t + 8, :] = value

        inputs.blocks(put)


class Flow:
    def __init__(self, acc, rate):
        self.acc, self.rate = acc, rate

    def settled(self, sv, c, at):
        above = jnp.maximum(sv[c, pl.ds(at + 7, 8), :], 0.0)
        below = jnp.minimum(sv[c, pl.ds(at + 9, 8), :], 0.0)
        return self.acc[c, rows8(at), :] + above - below

    def substep(self, begin, group, sv_in, sv_out, halves, strips, i):
        acc, lane = self.acc, lanes()
        start = pl.multiple_of(i * (8 * group), 8) + 8 * begin
        for g in range(group):
            at = start + 8 * g
            here = rows8(at)

            def cell(c):
                v = self.settled(sv_in, c, at)
                q = (v - 2.0) + pltpu.reciprocal(v, approx=True)
                down, across = self.rate(1, c, here) * q, self.rate(0, c, here) * q
                sv_out[c, rows8(at + 8), :] = down
                return v - jnp.abs(down + across), across

            heads = [cell(h * R) for h in halves]
            tails = [cell(h * R + R - 1) for h in halves]
            east = [pltpu.roll(jnp.maximum(x[1], 0.0), 1, 1) for x in tails]
            west = [pltpu.roll(jnp.minimum(x[1], 0.0), 127, 1) for x in heads]
            for c in strips:
                kept, across = cell(c)
                kept = kept + pltpu.roll(jnp.maximum(across, 0.0), 1, 1)
                acc[c, here, :] = kept - pltpu.roll(jnp.minimum(across, 0.0), 127, 1)
            for h in halves:
                this = heads[h]
                value = this[0] + jnp.where(lane == 0, east[1 - h], east[h])
                for b in range(1, R):
                    after = cell(h * R + b) if b < R - 1 else tails[h]
                    acc[h * R + b - 1, here, :] = value - jnp.minimum(after[1], 0.0)
                    value = after[0] + jnp.maximum(this[1], 0.0)
                    this = after
                acc[h * R + R - 1, here, :] = value - jnp.where(lane == 127, west[1 - h], west[h])


def strip_map():
    lane = lanes()
    fine = jnp.where(lane >= 64, lane - 64, lane + (NY * R - 64))
    return fine % R, fine // R % 128


def gathered(left, right, column):
    b_of, y_of = column
    near_left = lanes() < 64
    out = None
    for b in range(R):
        found = picked(jnp.where(near_left, left[b], right[b]), y_of)
        out = found if b == 0 else jnp.where(b_of == b, found, out)
    return out


def assemble_kernel(stw_in, sta_in, r02_in, r13_in, from_a, from_b, stw, sta, r02, r13, sr, pay_c, pay_d):
    group, gx, gy = info_of()
    even_x, even_y = lax.rem(gx, 2) == 0, lax.rem(gy, 2) == 0
    lane = lanes()

    @pl.when(group == 1)
    def _():
        at_a = jnp.where(even_x, ROWS - HALO, 0)
        at_b = ROWS - HALO - at_a

        def one(c):
            def join(v, h, w, to):
                stw[c, to, :] = v
                r02[c, to, :] = h
                r13[c, to, :] = w

            for t in range(OWN // 8):
                here = rows8(HALO + 8 * t)
                join(stw_in[c, here, :], r02_in[c, here, :], r13_in[c, here, :], here)
            for src, at in ((from_a, at_a), (from_b, at_b)):
                for t in range(HALO // 8):
                    v, h, w = (src[rows8((k * MAIN + c) * HALO + 8 * t), :] for k in range(3))
                    join(jnp.where(v == 0.0, 1.0, v), h, w, rows8(at + 8 * t))

        loop(MAIN, one)
        column = strip_map()

        def strips(t):
            for k, src in enumerate((stw, r02, r13)):
                found = []
                for half in range(2):
                    here = rows8(8 * t + 128 * half)
                    got = gathered([src[b, here, :] for b in range(R)], [src[R + b, here, :] for b in range(R)], column)
                    found.append(got)
                    if k == 0:
                        stw[MAIN, here, :] = got
                    else:
                        sr[2 * k - 2, here, :] = got
                one, two = found
                turned = pltpu.roll(two, 64, 1)
                to_left = jnp.where(lane >= 64, one, turned)
                to_right = jnp.where(lane < 64, one, turned)
                pay_c[rows8(k * 128 + 8 * t), :] = jnp.where(even_y, to_right, to_left)
                pay_d[rows8(k * 128 + 8 * t), :] = jnp.where(even_y, to_left, to_right)

        loop(16, strips)

    @pl.when(group == 0)
    def _():
        sub = lax.broadcasted_iota(jnp.int32, (8, 128), 0)

        def one(c):
            for h in range(2):
                for t in range(2):
                    here = slice(24 * h + 8 * t, 24 * h + 8 * t + 8)
                    sta[c, here, :] = sta_in[c, here, :]
                a, b = (x[rows8((c * 2 + h) * 8), :] for x in (from_a, from_b))
                above, below = jnp.where(even_x, b, a), jnp.where(even_x, a, b)
                sta[c, 24 * h + 16 : 24 * h + 24, :] = jnp.where(sub >= 4, above, below)

        loop(CH, one)

        def pack(i):
            k, t = i // 3, lax.rem(i, 3)
            to_left = jnp.zeros((8, 128), F32)
            to_right = to_left
            for j in range(32):
                c = jnp.minimum(32 * k + j, CH - 1)
                here = (lane >= 4 * j) & (lane < 4 * j + 4)
                west = sta[c, rows8(8 * t), :]
                east = sta[c, rows8(24 + 8 * t), :]
                to_left = jnp.where(here, pltpu.roll(west, 4 * j, 1), to_left)
                to_right = jnp.where(here, pltpu.roll(east, (4 * j + 4) % 128, 1), to_right)
            pay_c[rows8(k * 24 + 8 * t), :] = jnp.where(even_y, to_right, to_left)
            pay_d[rows8(k * 24 + 8 * t), :] = jnp.where(even_y, to_left, to_right)

        loop(12, pack)


def atmosphere_column(load, flux, regime, put):
    mixing = jnp.where(regime == 2.0, 0.4, 0.05)
    efficiency = jnp.where(regime == 0.0, 0.3, jnp.where(regime == 1.0, 0.6, 0.9))
    heat, damp = load(0) + flux, load(LEVELS) + flux
    heat_below, damp_below = heat, damp
    total = jnp.zeros((8, 128), F32)
    for k in range(LEVELS):
        last = k == LEVELS - 1
        heat_above = heat if last else load(k + 1)
        damp_above = damp if last else load(LEVELS + k + 1)
        t = heat + mixing * (heat_above + heat_below - 2.0 * heat)
        m = damp + mixing * (damp_above + damp_below - 2.0 * damp)
        capacity = (0.8 * math.exp(-3.0 * k / LEVELS)) * jnp.exp(0.3 * t)
        formed = efficiency * jnp.maximum(m - capacity, 0.0)
        put(k, t + 0.5 * formed)
        put(LEVELS + k, m - formed)
        total = total + formed
        heat_below, damp_below, heat, damp = heat, damp, heat_above, damp_above
    return total * (2.0 / LEVELS)


BANDS = ((0, 16, HALO), (16, 4, HALO + OWN), (20, 4, HALO - 4 * R))


def strip_rain(h0, h1, side, t):
    lane = lanes()
    here = slice(8 * t, 8 * t + 8)
    y = (lane + 16) // R - 8
    left = jnp.where(
        y < 0, picked(side[here], jnp.clip(128 + y, 0, 127)), picked(h0[here], jnp.clip(y, 0, 127))
    )
    y = (lane + (NY * R - 64)) // R
    right = jnp.where(
        y < NY, picked(h1[here], jnp.clip(y - 128, 0, 127)), picked(side[here], jnp.clip(y - NY, 0, 127))
    )
    return left, right


def strip_flux(left, right):
    lane = lanes()
    out = []
    for x, start in (
        (left, jnp.where(lane < 64, 64 + R * lane, 64 + R * (lane - 128))),
        (right, jnp.where(lane < 64, 64 + R * lane, 64 + R * (lane - 128))),
    ):
        back = lambda v, n: pltpu.roll(v, 128 - n, 1)
        two = x + back(x, 1)
        four = two + back(two, 2)
        ten = four + back(four, 4) + back(two, 8)
        out.append(picked(ten, jnp.clip(start, 0, 127)))
    return out


def route_kernel(step, *refs):
    opening, closing, merging = step == 0, step == STEPS - 1, step % 2 == 1
    if opening:
        stw, sta, r02, r13, sr_in, done, from_c, from_d, new, new_a, field, sr = refs[:12]
        acc, sv0, sv1, rain, sums, side_a = refs[12:]
        fld = None
    elif merging:
        stw, sta, r02, r13, sr, fld, acc, sv0, new_a, field = refs[:10]
        sv1, rain, sums = refs[10:]
    else:
        stw, sta, r02, r13, sr, fld, new, new_a, field = refs[:9]
        acc, sv0, sv1, rain, sums = refs[9:]
    group, _, gy = info_of()
    even_y = lax.rem(gy, 2) == 0
    lane = lanes()
    ranges = RANGES[step]
    first = ranges[0][0]
    count = TILES - 2 * first

    @pl.when(group == 0)
    def _():
        if opening:

            def side(i):
                k, t = i // 3, lax.rem(i, 3)
                c, d = from_c[rows8(k * 24 + 8 * t), :], from_d[rows8(k * 24 + 8 * t), :]
                west, east = jnp.where(even_y, d, c), jnp.where(even_y, c, d)
                for j in range(32):
                    side_a[32 * k + j, rows8(8 * t), :] = jnp.where(
                        lane < 4,
                        pltpu.roll(east, (128 - 4 * j) % 128, 1),
                        jnp.where(lane >= 124, pltpu.roll(west, 124 - 4 * j, 1), 0.0),
                    )

            loop(12, side)

        if closing:

            def own(i):
                h, t = i // 2, lax.rem(i, 2)
                here = rows8(24 * h + 8 * t)

                def put(c, value):
                    new_a[c, here, :] = value

                total = atmosphere_column(lambda c: sta[c, here, :], fld[here, :], sta[CH - 1, here, :], put)
                for u in range(2):

                    @pl.when(h == u)
                    def _():
                        field[rows8(8 * t), 128 * u : 128 * u + 128] = total

            loop(4, own)
        else:

            def block(load, here):
                def put(c, value):
                    new_a[c, here, :] = value

                regime = load(CH - 1)
                put(CH - 1, regime)
                flux = load(CH - 2) if opening else fld[here, :]
                field[here, :] = atmosphere_column(load, flux, regime, put)

            def inner(i):
                here = rows8(8 * i)
                block(lambda c: sta[c, here, :], here)

            def outer(t):
                block(lambda c: side_a[c, rows8(8 * t), :], rows8(48 + 8 * t))

            if opening:
                loop(6, inner)
                loop(3, outer)
            else:
                loop(9, inner)

    @pl.when(group == 1)
    def _():
        zero = jnp.zeros((8, 128), F32)
        if opening:

            def side(t):
                for half in range(2):
                    here = rows8(8 * t + 128 * half)
                    for k in range(3):
                        c, d = from_c[rows8(k * 128 + 8 * t), :], from_d[rows8(k * 128 + 8 * t), :]
                        west, east = jnp.where(even_y, d, c), jnp.where(even_y, c, d)
                        if half:
                            west, east = pltpu.roll(west, 64, 1), pltpu.roll(east, 64, 1)
                        if k == 0:
                            west = jnp.where(west == 0.0, 1.0, west)
                            east = jnp.where(east == 0.0, 1.0, east)
                        inner = sr_in[2 * k - 2, here, :] if k else stw[MAIN, here, :]
                        left = jnp.where(lane >= 64, inner, west)
                        right = jnp.where(lane < 64, inner, east)
                        if k == 0:
                            acc[MAIN, here, :] = left
                            acc[MAIN + 1, here, :] = right
                        else:
                            sr[2 * k - 2, here, :] = left
                            sr[2 * k - 1, here, :] = right

            loop(16, side)

        def of(main, k, c, here):
            return main[c, here, :] if c < MAIN else sr[2 * k + c - MAIN, here, :]

        if opening:

            def fill(t):
                for at in (8 * t, 8 * t + 8 * (TILES - EDGE_TILES)):
                    for c in range(MAIN):
                        acc[c, rows8(at), :] = stw[c, rows8(at), :]

        else:
            blocks = [fld[pl.ds(24 * i, 24), :] for i in range(3)]
            found = [strip_rain(*blocks, t) for t in range(3)]
            for at, n, fine in BANDS:
                if n == 16:
                    pieces = [b[:16] for b in blocks[:2]]
                    pieces += [jnp.concatenate([found[0][i], found[1][i]], 0) for i in range(2)]
                else:
                    cut = slice(at - 16, at - 12)
                    pieces = [b[at : at + 4] for b in blocks[:2]] + [found[2][i][cut] for i in range(2)]
                for i, piece in enumerate(pieces):
                    for a in range(R):
                        rain[i, pl.ds(fine + a, n, stride=R), :] = piece

            def fill(t):
                for u in range(2):
                    at = 16 * t + 8 * first + 8 * u
                    here = rows8(at)
                    for c in range(NCH):
                        fall = rain[c // R if c < MAIN else c - MAIN + 2, here, :]
                        rate = jnp.abs(of(r02, 0, c, here) + of(r13, 1, c, here))
                        share = 0.275 + 1.75 * rate
                        acc[c, here, :] = stw[c, here, :] + share * fall
                        sv0[c, rows8(at + 8), :] = zero

        loop(EDGE_TILES if opening else count // 2, fill)

        def clear(t):
            for c in range(NCH):
                sv0[c, rows8(8 * (t + first)), :] = zero

        if opening:
            loop(count + 2, clear)
        for c in range(NCH):
            if not opening:
                sv0[c, rows8(8 * first), :] = zero
                sv0[c, rows8(8 * (first + count + 1)), :] = zero
            sv1[c, rows8(8 * first), :] = zero
            sv1[c, rows8(8 * (first + count + 1)), :] = zero

        flow = Flow(acc, lambda k, c, here: of((r02, r13)[k], k, c, here))
        strips = (MAIN, MAIN + 1)
        if opening:
            for c in range(MAIN):
                sv1[c, rows8(8 * (EDGE_TILES + 1)), :] = zero
                sv1[c, rows8(8 * (TILES - EDGE_TILES)), :] = zero

            for trim, substeps in ((0, 8), (1, 4)):

                def pair(_):
                    size = EDGE_TILES - 2 * trim
                    for sv in ((sv0, sv1), (sv1, sv0)):
                        flow.substep(trim, size, *sv, range(2), (), 0)
                        flow.substep(TILES - trim - size, size, *sv, range(2), (), 0)
                        loop(2, functools.partial(flow.substep, 0, TILES // 2, *sv, (), strips))

                loop(substeps // 2, pair)
        else:
            for begin, size, substeps in ranges:

                def pair(_):
                    times = (TILES - 2 * begin) // size
                    loop(times, functools.partial(flow.substep, begin, size, sv0, sv1, range(2), strips))
                    loop(times, functools.partial(flow.substep, begin, size, sv1, sv0, range(2), strips))

                loop(substeps // 2, pair)

        start = HALO // 8 if closing else RANGES[step + 1][0][0]

        def tally(at):
            here = rows8(at)
            for h in range(2):
                total = None
                for c in range(h * R, h * R + R):
                    v = flow.settled(sv0, c, at)
                    if opening:
                        v = jnp.where(early_rows(at), done[c, here, :], v)
                    if not merging:
                        new[c, here, :] = 0.9 * v + 0.1
                    total = v if total is None else total + v
                sums[h, here, :] = total - float(R)
            for c in (MAIN, MAIN + 1):
                v = flow.settled(sv0, c, at)
                if not merging:
                    new[c, here, :] = 0.9 * v + 0.1
                sums[c - MAIN + 2, here, :] = v - 1.0

        def two(t):
            for u in range(2):
                tally(16 * t + 8 * start + 8 * u)

        loop(TILES // 2 - start, two)
        scale = 0.1 / (2.0 * R * R)
        pooled = []
        for at, n, fine in BANDS[: 1 if closing else 3]:
            parts = []
            for i in range(4):
                total = sums[i, pl.ds(fine, n, stride=R), :]
                for a in range(1, R):
                    total = total + sums[i, pl.ds(fine + a, n, stride=R), :]
                parts.append(total * scale)
            pooled.append(parts)
        if not closing:
            for i in range(4):
                rain[i, 0:16, :] = pooled[0][i]
                rain[i, 16:20, :] = pooled[1][i]
                rain[i, 20:24, :] = pooled[2][i]
        for t in range(2 if closing else 3):
            rows = slice(8 * t, 8 * t + 8)
            if closing:
                h0, h1, west, east = (pooled[0][i][rows] for i in range(4))
            else:
                h0, h1, west, east = (rain[i, rows, :] for i in range(4))
            west, east = strip_flux(west, east)
            h0 = jnp.where(lane < 3, west, h0)
            h1 = jnp.where(lane >= 125, east, h1)
            if closing:
                field[rows, 0:128] = h0
                field[rows, 128:256] = h1
            else:
                field[rows, :] = h0
                field[24 + 8 * t : 32 + 8 * t, :] = h1
                field[48 + 8 * t : 56 + 8 * t, :] = jnp.where(lane < 64, east, west)


def early_rows(at):
    row = lax.broadcasted_iota(jnp.int32, (8, 128), 0) + at
    return (row >= HALO + SUB) & (row < ROWS - HALO - SUB)


def settle_kernel(step, *refs):
    closing = step == STEPS - 1
    if closing:
        acc, sv0, sta, out, last = refs
    else:
        acc, sv0, new = refs
    group, _, _ = info_of()
    lane = lanes()

    @pl.when(group == 1)
    def _():
        flow = Flow(acc, None)
        column = strip_map()
        start = HALO // 8 if closing else RANGES[step + 1][0][0]
        near_left = lane < 64

        def finish(at):
            here = rows8(at)
            v = [flow.settled(sv0, c, at) for c in range(NCH)]
            strip = jnp.where(near_left, v[MAIN + 1], v[MAIN])
            if not closing:
                inner = gathered(v[:R], v[R:MAIN], column)
            for b in range(R):
                place = R * lane + b
                index = jnp.where(near_left, place + 64, place - (128 * R - 64))
                got = picked(strip, jnp.clip(index, 0, 127))
                v[b] = jnp.where(place < 2 * SUB, got, v[b])
                v[R + b] = jnp.where(index >= 64 - 2 * SUB, jnp.where(near_left, v[R + b], got), v[R + b])
            if not closing:
                v[MAIN] = jnp.where(lane >= 64 + 2 * SUB, inner, v[MAIN])
                v[MAIN + 1] = jnp.where(lane < 64 - 2 * SUB, inner, v[MAIN + 1])
            if closing:
                for c in range(MAIN):
                    last[c, rows8(at - HALO), :] = 0.45 * (v[c] - 1.0)
            else:
                for c in range(NCH):
                    new[c, here, :] = 0.9 * v[c] + 0.1

        def two(t):
            for u in range(2):
                finish(16 * t + 8 * start + 8 * u)

        loop(TILES // 2 - start, two)
        if closing:

            def lay(a):
                for b in range(R):
                    for h in range(2):
                        out[a * R + b, :, 128 * h : 128 * h + 128] = last[h * R + b, pl.ds(a, NX, stride=R), :]

            loop(R, lay)

    if closing:

        @pl.when(group == 0)
        def _():
            def copy(i):
                for u in range(10):
                    for h in range(2):
                        out[i * 10 + u, :, 128 * h : 128 * h + 128] = sta[i * 10 + u, 24 * h : 24 * h + 16, :]

            loop(R, copy)


def call(kernel, args, out, scratch=(), hbm=False, out_hbm=False, limit=16, flops=0):
    return pl.pallas_call(
        kernel,
        out_shape=[jax.ShapeDtypeStruct(s, F32) for s in out],
        in_specs=[pl.BlockSpec(memory_space=pltpu.HBM if hbm else pltpu.VMEM)] * len(args),
        out_specs=[pl.BlockSpec(memory_space=pltpu.HBM if out_hbm else pltpu.VMEM)] * len(out),
        scratch_shapes=[pltpu.VMEM(x, F32) if isinstance(x, tuple) else x for x in scratch],
        compiler_params=pltpu.CompilerParams(vmem_limit_bytes=limit * MIB),
        cost_estimate=pl.CostEstimate(flops=flops, bytes_accessed=5 * MIB, transcendentals=0) if flops else None,
    )(*args)


def pairs(axis, odd):
    n = lax.axis_size(axis)
    found = [(i, i + 1) for i in range(odd, n - 1, 2)]
    return found + [(j, i) for i, j in found]


def on_device(domain_state, coupling_field, regime, land_class, flow_code):
    tile = (2 * LEVELS, NX, NY)
    full, water, air = (MAIN, ROWS, 128), (NCH, ROWS, 128), (CH, 72, 128)
    strips, rim, small = (4, ROWS, 128), (384, 128), (72, 128)
    flows, inner_flows = (NCH, SVR, 128), (MAIN, SVR, 128)
    args = (domain_state[0], coupling_field[0], regime, land_class, flow_code)
    held = (
        tile,
        (NX, NY),
        pltpu.VMEM((NX, NY), jnp.int32),
        pltpu.VMEM(tile, jnp.int32),
        pltpu.VMEM(tile, jnp.int32),
        pltpu.SemaphoreType.DMA((3, R)),
        pltpu.SemaphoreType.DMA((2,)),
    )
    edge = (3 * EDGE, 128)
    pay_a, pay_b = call(
        prep_kernel,
        args,
        (edge, edge),
        held + (edge, edge, (3 * MAIN, OWN, 128), pltpu.SemaphoreType.DMA((2, 3))),
        hbm=True,
        out_hbm=True,
        limit=56,
    )
    from_a = lax.ppermute(pay_a, "gx", pairs("gx", 0))
    from_b = lax.ppermute(pay_b, "gx", pairs("gx", 1))
    stw, sta, r02, r13, done = call(
        early_kernel,
        args,
        (full, air, full, full, full),
        held + (full, inner_flows, inner_flows),
        hbm=True,
        limit=17,
        flops=200_000_000,
    )
    stw, sta, r02, r13, sr, pay_c, pay_d = call(
        assemble_kernel, (stw, sta, r02, r13, from_a, from_b), (water, air, full, full, strips, rim, rim)
    )
    from_c = lax.ppermute(pay_c, "gy", pairs("gy", 0))
    from_d = lax.ppermute(pay_d, "gy", pairs("gy", 1))
    spare = (flows, (4, ROWS, 128), (4, ROWS, 128))
    scratch = (water, flows) + spare
    for step in range(STEPS):
        kernel = functools.partial(route_kernel, step)
        settle = functools.partial(settle_kernel, step)
        if step == 0:
            stw, sta, field, sr = call(
                kernel,
                (stw, sta, r02, r13, sr, done, from_c, from_d),
                (water, air, small, strips),
                scratch + ((128, 24, 128),),
            )
        elif step % 2 == 0:
            stw, sta, field = call(kernel, (stw, sta, r02, r13, sr, field), (water, air, small), scratch)
        else:
            shape = (NX, NY) if step == STEPS - 1 else small
            acc, sv, sta, field = call(
                kernel, (stw, sta, r02, r13, sr, field), (water, flows, air, shape), spare
            )
        field = lax.ppermute(field, "group", [(0, 1), (1, 0)])
        if step == STEPS - 1:
            out = call(settle, (acc, sv, sta), (tile,), ((MAIN, OWN, 128),), flops=50_000_000)[0]
        elif step % 2:
            stw = call(settle, (acc, sv), (water,), flops=50_000_000)[0]
    return (out[None], field[None])


def solution(mesh):
    return jax.shard_map(
        on_device,
        mesh=mesh,
        in_specs=(
            P("group", None, "gx", "gy"),
            P("group", "gx", "gy"),
            P("gx", "gy"),
            P(None, "gx", "gy"),
            P(None, "gx", "gy"),
        ),
        out_specs=(P("group", None, "gx", "gy"), P("group", "gx", "gy")),
        check_vma=False,
    )
```
